32 devices in a mesh: groups: 2 (over y), wide: 4 (over z), narrow: 4 (over x, core).
Axes of the slice: x: 2, y: 2, z: 4, core: 2. Of those that a mesh axis runs over, the one named last changes fastest.
Arguments:
- inputs: bfloat16 [40, 2, 8192], P('groups', None, 'narrow'), parts along dimension 0, may hold values from -6 to 6
- xz_weight: bfloat16 [8192, 2, 16384], P('narrow', None, 'wide'), may hold values from -0.0625 to 0.0625
- bc_weight: bfloat16 [8192, 4096], P('narrow', 'wide'), may hold values from -0.0625 to 0.0625
- dt_weight: bfloat16 [8192, 256], P('narrow', 'wide'), may hold values from -0.0625 to 0.0625
- conv_x_weight: bfloat16 [4, 256, 64], P(None, 'wide', 'narrow'), may hold values from -3 to 3
- conv_x_bias: bfloat16 [256, 64], P('wide', 'narrow'), may hold values from -3 to 3
- conv_bc_weight: bfloat16 [4, 4096], P(None, 'wide'), may hold values from -3 to 3
- conv_bc_bias: bfloat16 [4096], P('wide'), may hold values from -3 to 3
- conv_x_state: bfloat16 [40, 3, 256, 64], P('groups', None, 'wide', 'narrow'), parts along dimension 0, may hold values from -6 to 6
- conv_bc_state: bfloat16 [40, 3, 4096], P('groups', None, 'wide'), parts along dimension 0, may hold values from -6 to 6
- dt_bias: float32 [256], P('wide'), may hold values from -4 to 0
- a_log: float32 [256], P('wide'), may hold values from 0 to 2.5
- d_skip: float32 [256], P('wide'), may hold values from 0.5 to 2
- norm_weight: bfloat16 [256, 64], P('wide', 'narrow'), may hold values from 0.099609375 to 1.8984375
- out_weight: bfloat16 [256, 64, 8192], P(None, 'narrow', 'wide'), may hold values from -0.046875 to 0.046875
- ssm_state: float32 [40, 256, 64, 256], P('groups', 'wide', 'narrow'), parts along dimension 0, may hold values from -4 to 4
Outputs:
- layer_out: bfloat16 [40, 2, 8192], P('groups', None, ('wide', 'narrow')), parts along dimension 0
- new_ssm_state: float32 [40, 256, 64, 256], P('groups', 'wide', 'narrow'), parts along dimension 0
- new_conv_x: bfloat16 [40, 3, 256, 64], P('groups', None, 'wide', 'narrow'), parts along dimension 0
- new_conv_bc: bfloat16 [40, 3, 4096], P('groups', None, 'wide'), parts along dimension 0
The draws below stay inside these ranges and needn't reach their ends.
There are 2 independent parts, one for each index of `groups`. The reference program is written for one: setup_inputs(seed, part) draws one part's arguments, and reference() takes and returns one part's arrays. A program takes and returns all parts, laid end to end along the dimension named above; an argument that names none is the same for every part. Nothing has to cross between parts.
All inputs are finite; a program needn't handle non-finite values.
Results may differ from the reference program's by a relative error of at most 0.015.
Values may be sent and summed in bfloat16 or wider, within the bound.
No kernel may reach another device: no remote copies, remote signals or barrier semaphores. Data moves between devices by JAX's collectives and lax.ppermute only.
A program may use at most 192 MiB of HBM per device.

```python
import math
import jax
import jax.numpy as jnp
from jax import lax

D = 8192
HEADS = 256
HEAD_DIM = 64
STATE = 256
NGROUPS = 8
CONV = 4
SEQS = 20
INNER = 16384
BCW = 4096


def steps_of(key, shape, split, low, largest):
    def one(dim, blocks):
        steps = jax.random.uniform(jax.random.fold_in(jax.random.fold_in(key, 6), dim), (blocks,), jnp.float32, low / len(split), largest / len(split))
        return jnp.repeat(jnp.exp(steps), shape[dim] // blocks).reshape((-1,) + (1,) * (len(shape) - dim - 1))

    gain = one(*split[0])
    for cut in split[1:]:
        gain = gain * one(*cut)
    return gain


def centred(own_key, extent, spread, limit, shards=(), kind=jnp.bfloat16):
    factor_of = steps_of(own_key, extent, shards, -0.22, 0.18) if shards else 1.0
    array = jax.random.normal(own_key, extent, jnp.float32) * spread * factor_of
    return jnp.minimum(jnp.maximum(array, -limit), limit).astype(kind)


def setup_inputs(seed: int = 0, part: int = 0) -> dict:
    seeds = jax.random.split(jax.random.key(seed), 17)
    part_splits = jax.random.split(jax.random.fold_in(seeds[16], part), 17)
    inputs = centred(part_splits[0], (SEQS, 2, D), 1.0, 6.0, ((2, 4),))
    xz_weight = centred(seeds[1], (D, 2, INNER), D ** -0.5, 0.0625, ((0, 4), (2, 4)))
    bc_weight = centred(seeds[2], (D, BCW), D ** -0.5, 0.0625, ((0, 4), (1, 4)))
    dt_weight = centred(seeds[3], (D, HEADS), D ** -0.5, 0.0625, ((0, 4), (1, 4)))
    conv_x_weight = centred(seeds[4], (CONV, HEADS, HEAD_DIM), CONV ** -0.5, 3.0, ((1, 4), (2, 4)))
    conv_x_bias = centred(seeds[5], (HEADS, HEAD_DIM), 0.5, 3.0, ((0, 4), (1, 4)))
    conv_bc_weight = centred(seeds[6], (CONV, BCW), CONV ** -0.5, 3.0, ((1, 4),))
    conv_bc_bias = centred(seeds[7], (BCW,), 0.5, 3.0, ((0, 4),))
    conv_x_state = centred(part_splits[8], (SEQS, CONV - 1, HEADS, HEAD_DIM), 1.0, 6.0, ((2, 4), (3, 4)))
    conv_bc_state = centred(part_splits[9], (SEQS, CONV - 1, BCW), 1.0, 6.0, ((2, 4),))
    dt_bias = jnp.clip(-4.0 + 4.0 * jax.random.uniform(seeds[10], (HEADS,), jnp.float32) ** steps_of(seeds[10], (HEADS,), ((0, 4),), -0.2, 0.2), -4.0, 0.0)
    a_log = jnp.clip(2.5 * jax.random.uniform(seeds[11], (HEADS,), jnp.float32) ** steps_of(seeds[11], (HEADS,), ((0, 4),), -0.2, 0.2), 0.0, 2.5)
    d_skip = jnp.clip(jnp.exp(math.log(2.0) - 1.3862944 * jax.random.uniform(seeds[12], (HEADS,), jnp.float32) ** steps_of(seeds[12], (HEADS,), ((0, 4),), -0.2, 0.2)), 0.5, 2.0)
    norm_weight = jnp.clip(1.0 + 0.18 * jax.random.normal(seeds[13], (HEADS, HEAD_DIM), jnp.float32), 0.099609375, 1.8984375).astype(jnp.bfloat16)
    out_weight = centred(seeds[14], (HEADS, HEAD_DIM, D), INNER ** -0.5, 0.046875, ((1, 4), (2, 4)))
    ssm_state = centred(part_splits[15], (SEQS, HEADS, HEAD_DIM, STATE), 0.5, 4.0, ((1, 4), (2, 4)), jnp.float32)
    return dict(inputs=inputs, xz_weight=xz_weight, bc_weight=bc_weight, dt_weight=dt_weight, conv_x_weight=conv_x_weight, conv_x_bias=conv_x_bias, conv_bc_weight=conv_bc_weight, conv_bc_bias=conv_bc_bias, conv_x_state=conv_x_state, conv_bc_state=conv_bc_state, dt_bias=dt_bias, a_log=a_log, d_skip=d_skip, norm_weight=norm_weight, out_weight=out_weight, ssm_state=ssm_state)


EPSILON = 1e-05

def conv_tokens(history, fresh_vals, tap_weights, offset):
    window = jnp.concatenate([history, fresh_vals], axis=1)
    outputs = []
    for token_idx in range(2):
        summed = offset.astype(jnp.float32)
        for tap_idx in range(tap_weights.shape[0]):
            summed = summed + tap_weights[tap_idx].astype(jnp.float32) * window[:, token_idx + tap_idx].astype(jnp.float32)
        outputs.append(jax.nn.silu(summed))
    return (jnp.stack(outputs, axis=1), window[:, 2:])

def advance(ssm_now, x_tok, b_tok, c_tok, dt_tok, dt_bias, a_log, d_skip):
    step_size = jax.nn.softplus(dt_tok.astype(jnp.float32) + dt_bias)
    decay_now = jnp.exp(-step_size * jnp.exp(a_log))
    inject = (step_size[:, :, None] * x_tok)[..., None] * b_tok[:, :, None, :]
    ssm_now = decay_now[:, :, None, None] * ssm_now + inject
    readout = lax.optimization_barrier(jnp.sum(ssm_now * c_tok[:, :, None, :], axis=-1)) + d_skip[None, :, None] * x_tok
    return (ssm_now, readout)

def reference(inputs, xz_weight, bc_weight, dt_weight, conv_x_weight, conv_x_bias, conv_bc_weight, conv_bc_bias, conv_x_state, conv_bc_state, dt_bias, a_log, d_skip, norm_weight, out_weight, ssm_state):
    tok_rows = inputs.reshape(SEQS * 2, D)
    xz_proj = jnp.dot(tok_rows, xz_weight.reshape(D, 2 * INNER), preferred_element_type=jnp.float32).astype(jnp.bfloat16)
    xz_proj = xz_proj.reshape(SEQS, 2, 2, HEADS, HEAD_DIM)
    gate_vals = xz_proj[:, :, 0]
    x_proj = xz_proj[:, :, 1]
    bc_proj = jnp.dot(tok_rows, bc_weight, preferred_element_type=jnp.float32).astype(jnp.bfloat16).reshape(SEQS, 2, BCW)
    dt_proj = jnp.dot(tok_rows, dt_weight, preferred_element_type=jnp.float32).astype(jnp.bfloat16).reshape(SEQS, 2, HEADS)
    x_conv, new_conv_x = conv_tokens(conv_x_state, x_proj, conv_x_weight, conv_x_bias)
    bc_conv, new_conv_bc = conv_tokens(conv_bc_state, bc_proj, conv_bc_weight, conv_bc_bias)
    bc_groups = bc_conv.reshape(SEQS, 2, NGROUPS, 2, STATE)
    b_heads = jnp.repeat(bc_groups[:, :, :, 0], HEADS // NGROUPS, axis=2)
    c_heads = jnp.repeat(bc_groups[:, :, :, 1], HEADS // NGROUPS, axis=2)
    ssm_now = ssm_state
    readouts = []
    for token_idx in range(2):
        ssm_now, readout = advance(ssm_now, x_conv[:, token_idx], b_heads[:, token_idx], c_heads[:, token_idx], dt_proj[:, token_idx], dt_bias, a_log, d_skip)
        readouts.append(readout)
    y_all = jnp.stack(readouts, axis=1)
    gated_out = y_all * jax.nn.silu(gate_vals.astype(jnp.float32))
    grouped = gated_out.reshape(SEQS, 2, NGROUPS, HEADS // NGROUPS * HEAD_DIM)
    group_sum = lax.optimization_barrier(jnp.sum(grouped * grouped, axis=-1))
    inverse = lax.rsqrt(group_sum / (HEADS // NGROUPS * HEAD_DIM) + EPSILON)
    normed = (grouped * inverse[..., None]).reshape(SEQS, 2, HEADS, HEAD_DIM) * norm_weight.astype(jnp.float32)
    normed = normed.astype(jnp.bfloat16)
    layer_out = jnp.dot(normed.reshape(SEQS * 2, INNER), out_weight.reshape(INNER, D), preferred_element_type=jnp.float32)
    layer_out = layer_out.astype(jnp.bfloat16).reshape(SEQS, 2, D)
    return (layer_out, ssm_now, new_conv_x, new_conv_bc)
```

```python
import functools

import jax
import jax.numpy as jnp
from jax import lax
from jax.experimental import pallas as pl
from jax.experimental.pallas import tpu as pltpu
from jax.sharding import PartitionSpec as P

HEADS = 256
HEAD_DIM = 64
STATE = 256
NGROUPS = 8
LANES = 128
MIB = 2**20

EPSILON = 1e-05

F32 = jnp.float32
BF16 = jnp.bfloat16
VMEM_SPEC = pl.BlockSpec(memory_space=pltpu.VMEM)
SMEM_SPEC = pl.BlockSpec(memory_space=pltpu.SMEM)
ANY_SPEC = pl.BlockSpec(memory_space=pl.ANY)


def exchanged(value, axis, mask):
    return lax.ppermute(value, axis, [(i, i ^ mask) for i in range(lax.axis_size(axis))])


def from_all(value, axis):
    return [value] + [exchanged(value, axis, mask) for mask in range(1, lax.axis_size(axis))]


def silu(value):
    return value / (1.0 + jnp.exp(-value))


def iota(shape, dim):
    return lax.broadcasted_iota(jnp.int32, shape, dim)


def params(mib, **more):
    return pltpu.CompilerParams(vmem_limit_bytes=mib * MIB, **more)


def cost(flops, nbytes):
    return pl.CostEstimate(flops=int(flops), bytes_accessed=int(nbytes), transcendentals=0)


def small_proj_kernel(x_ref, bc_ref, dt_ref, part_ref, spread_ref, *, depth):
    rows, feats = x_ref.shape
    bc_cols = bc_ref.shape[1]
    dt_cols = dt_ref.shape[0]
    part_ref[:, :bc_cols] = jnp.dot(x_ref[...], bc_ref[...], preferred_element_type=F32).astype(BF16)
    dt_part = lax.dot_general(x_ref[...], dt_ref[...], (((1,), (1,)), ((), ())), preferred_element_type=F32)
    pad = jnp.zeros((rows, part_ref.shape[1] - bc_cols - dt_cols), F32)
    part_ref[:, bc_cols:] = jnp.concatenate([dt_part, pad], axis=1).astype(BF16)
    place = iota((depth, 2 * depth), 1) - 2 * iota((depth, 2 * depth), 0)
    for z in range(2):
        one_hot = (place == z).astype(F32).astype(BF16)
        for i in range(feats // depth):
            spread = jnp.dot(x_ref[:, i * depth : (i + 1) * depth], one_hot, preferred_element_type=F32)
            spread_ref[i, z * rows : (z + 1) * rows] = spread.astype(BF16)


def small_proj(x, bc_weight, dt_weight_t, depth):
    rows, feats = x.shape
    bc_cols = bc_weight.shape[1]
    return pl.pallas_call(
        functools.partial(small_proj_kernel, depth=depth),
        out_shape=(
            jax.ShapeDtypeStruct((rows, bc_cols + LANES), BF16),
            jax.ShapeDtypeStruct((feats // depth, 2 * rows, 2 * depth), BF16),
        ),
        in_specs=[VMEM_SPEC] * 3,
        out_specs=(VMEM_SPEC, VMEM_SPEC),
        compiler_params=params(24),
        cost_estimate=cost(2 * rows * feats * (bc_cols + 3 * depth), 2 * feats * bc_cols),
        name="small_proj",
    )(x, bc_weight, dt_weight_t)


def big_proj_kernel(me_ref, x_ref, w_ref, *refs, depth, slots, narrow, chan):
    outs = refs[:narrow]
    wide_tiles, tiles, total, chunks, tile_sem, flat_sem = refs[narrow:]
    steps = w_ref.shape[0] // depth
    blocks = w_ref.shape[1]

    def start(i):
        for block in range(blocks):
            pltpu.make_async_copy(
                w_ref.at[pl.ds(i * depth, depth), block], wide_tiles.at[i % slots, block], tile_sem.at[i % slots]
            ).start()

    def wait(i):
        held = wide_tiles.at[i % slots]
        pltpu.make_async_copy(held, held, tile_sem.at[i % slots]).wait()

    def flat_copy(i):
        source = wide_tiles.at[i % slots].reshape(blocks * 2 * depth, LANES)
        return pltpu.make_async_copy(source, tiles.at[i % 2], flat_sem.at[i % 2])

    for i in range(min(slots, steps)):
        start(i)
    total[...] = jnp.zeros_like(total)
    span = narrow * LANES
    column = iota((span, span), 0)
    target = (column % HEAD_DIM) // chan * LANES + column // HEAD_DIM * chan + column % chan
    mover = (target == iota((span, span), 1)).astype(F32).astype(BF16)
    wait(0)
    flat_copy(0).start()
    for i in range(steps):
        flat_copy(i).wait()
        if i + slots < steps:
            start(i + slots)
        if i + 1 < steps:
            wait(i + 1)
            flat_copy(i + 1).start()
        pair = 2 if blocks % 2 == 0 else 1
        for block in range(0, blocks, pair):
            weight = jnp.concatenate(
                [tiles[i % 2, (block + j) * 2 * depth : (block + j + 1) * 2 * depth] for j in range(pair)], axis=1
            )
            columns = slice(block * LANES, (block + pair) * LANES)
            total[:, columns] += jnp.dot(x_ref[i], weight, preferred_element_type=F32)
    for q in range(total.shape[1] // span):
        moved = jnp.dot(total[:, q * span : (q + 1) * span].astype(BF16), mover, preferred_element_type=F32)
        for n in range(narrow):
            chunks[n, :, q * LANES : (q + 1) * LANES] = moved[:, n * LANES : (n + 1) * LANES].astype(BF16)
    for mask in range(narrow):
        outs[mask][...] = chunks[me_ref[1] ^ mask]


def big_proj(me, spread, weight, depth, narrow, chan):
    feats, _, cols = weight.shape
    rows = spread.shape[1]
    blocks = cols // LANES
    slots = 3
    by_block = weight.reshape(feats, 2, blocks, LANES).transpose(0, 2, 1, 3)
    return pl.pallas_call(
        functools.partial(big_proj_kernel, depth=depth, slots=slots, narrow=narrow, chan=chan),
        out_shape=[jax.ShapeDtypeStruct((rows, cols // narrow), BF16)] * narrow,
        in_specs=[SMEM_SPEC, VMEM_SPEC, ANY_SPEC],
        out_specs=[VMEM_SPEC] * narrow,
        scratch_shapes=[
            pltpu.VMEM((slots, blocks, depth, 2, LANES), BF16),
            pltpu.VMEM((2, blocks * 2 * depth, LANES), BF16),
            pltpu.VMEM((rows, cols), F32),
            pltpu.VMEM((narrow, rows, cols // narrow), BF16),
            pltpu.SemaphoreType.DMA((slots,)),
            pltpu.SemaphoreType.DMA((2,)),
        ],
        compiler_params=params(32),
        cost_estimate=cost(2 * rows * feats * 2 * cols, 4 * feats * cols),
        name="big_proj",
    )(me, spread, by_block)


def conv_pair(history, fresh, taps, offset):
    window = list(history) + list(fresh)
    outputs = []
    for token in range(2):
        summed = offset
        for tap in range(4):
            summed = summed + taps[tap : tap + 1] * window[token + tap]
        outputs.append(silu(summed))
    return outputs


def bc_conv_kernel(*refs, parts, seqs):
    part_refs = refs[:parts]
    history_ref, taps_ref, offset_ref, conv_ref, kept_ref, dt_ref = refs[parts:]
    summed = part_refs[0][...].astype(F32)
    for part_ref in part_refs[1:]:
        summed = summed + part_ref[...].astype(F32)
    half = summed.shape[0] // 2
    cols = taps_ref.shape[1]
    proj = summed.astype(BF16).astype(F32)
    dt_ref[...] = proj[:, cols:]
    fresh = [proj[:seqs, :cols], proj[half : half + seqs, :cols]]
    history = [history_ref[i].astype(F32) for i in range(3)]
    conv_ref[...] = jnp.zeros_like(conv_ref)
    for token, value in enumerate(conv_pair(history, fresh, taps_ref[...].astype(F32), offset_ref[...].astype(F32))):
        conv_ref[token * half : token * half + seqs] = value
    kept_ref[0] = history_ref[2]
    kept_ref[1] = fresh[0].astype(BF16)
    kept_ref[2] = fresh[1].astype(BF16)


def bc_conv(parts, history, taps, offset):
    rows = parts[0].shape[0]
    cols = taps.shape[1]
    return pl.pallas_call(
        functools.partial(bc_conv_kernel, parts=len(parts), seqs=history.shape[1]),
        out_shape=(
            jax.ShapeDtypeStruct((rows, cols), F32),
            jax.ShapeDtypeStruct(history.shape, BF16),
            jax.ShapeDtypeStruct((rows, LANES), F32),
        ),
        in_specs=[VMEM_SPEC] * (len(parts) + 3),
        out_specs=(VMEM_SPEC,) * 3,
        compiler_params=params(8),
        cost_estimate=cost(30 * rows * cols, 8 * rows * cols),
        name="bc_conv",
    )(*parts, history, taps, offset)


def state_read_kernel(bc_ref, state_ref, read_ref, *, groups):
    step = pl.program_id(0)
    count, rows, _ = state_ref.shape
    half = bc_ref.shape[0] // 2
    span = rows // groups

    @pl.when(step == 0)
    def _():
        read_ref[...] = jnp.zeros_like(read_ref)

    for j in range(count):
        seq = step * count + j
        for g in range(groups):
            cols = slice((2 * g + 1) * STATE, (2 * g + 2) * STATE)
            both = jnp.concatenate([bc_ref[pl.ds(t * half + seq, 1), cols] for t in range(2)], axis=0)
            held = state_ref[j, g * span : (g + 1) * span].astype(BF16)
            out = lax.dot_general(both.astype(BF16), held, (((1,), (1,)), ((), ())), preferred_element_type=F32)
            for t in range(2):
                read_ref[pl.ds(t * half + seq, 1), g * span : (g + 1) * span] = out[t : t + 1]


def state_read(bc, state, groups, count):
    seqs, rows, _ = state.shape
    return pl.pallas_call(
        functools.partial(state_read_kernel, groups=groups),
        grid=(seqs // count,),
        out_shape=jax.ShapeDtypeStruct((bc.shape[0], rows), F32),
        in_specs=[
            pl.BlockSpec(bc.shape, lambda i: (0, 0)),
            pl.BlockSpec((count, rows, STATE), lambda i: (i, 0, 0)),
        ],
        out_specs=pl.BlockSpec((bc.shape[0], rows), lambda i: (0, 0)),
        compiler_params=params(16),
        cost_estimate=cost(4 * state.size, 4 * state.size),
        name="state_read",
    )(bc, state)


def readout_kernel(*refs, parts, seqs, groups, heads, chan):
    part_refs = refs[:parts]
    history_ref, small_ref, offset_ref, gain_ref, read_ref, bc_ref, dt_ref, heads_ref = refs[parts : parts + 8]
    sent_ref, fresh_ref, scale_ref, decay_ref = refs[parts + 8 :]
    summed = part_refs[0][...].astype(F32)
    for part_ref in part_refs[1:]:
        summed = summed + part_ref[...].astype(F32)
    proj = summed.astype(BF16).astype(F32)
    half = proj.shape[0] // 4
    width = proj.shape[1]
    gates = [proj[:half], proj[half : 2 * half]]
    fresh = [proj[2 * half : 3 * half], proj[3 * half :]]
    fresh_ref[...] = proj[2 * half :].astype(BF16)
    history = [history_ref[i * half : (i + 1) * half].astype(F32) for i in range(3)]
    x = conv_pair(history, fresh, small_ref[...].astype(F32), offset_ref[...].astype(F32))

    bias, rate, skip = heads_ref[0:1], jnp.exp(heads_ref[1:2]), heads_ref[2:3]
    raw = dt_ref[:, :heads] + bias
    step = jnp.maximum(raw, 0.0) + jnp.log1p(jnp.exp(-jnp.abs(raw)))
    decay = jnp.exp(-step * rate)
    decay_ref[...] = decay[:half] * decay[half:]
    repeat = (iota((heads, width), 1) // chan == iota((heads, width), 0)).astype(F32)
    packed = jnp.concatenate([step, decay, jnp.broadcast_to(skip, (8, heads))], axis=0)
    spread = jnp.dot(packed, repeat, preferred_element_type=F32, precision=lax.Precision.HIGHEST)
    steps = [spread[:half], spread[half : 2 * half]]
    decays = [spread[2 * half : 3 * half], spread[3 * half : 4 * half]]
    skips = spread[4 * half : 4 * half + 1]

    span = width // groups

    def dots(b_token, c_token):
        out = []
        for g in range(groups):
            b = bc_ref[b_token * half : (b_token + 1) * half, 2 * g * STATE : (2 * g + 1) * STATE]
            c = bc_ref[c_token * half : (c_token + 1) * half, (2 * g + 1) * STATE : (2 * g + 2) * STATE]
            out.append(jnp.broadcast_to(jnp.sum(b * c, axis=1, keepdims=True), (half, span)))
        return jnp.concatenate(out, axis=1)

    first = steps[0] * x[0]
    second = steps[1] * x[1]
    carried = decays[1] * first
    y = [
        decays[0] * read_ref[:half] + first * dots(0, 0) + skips * x[0],
        decays[0] * decays[1] * read_ref[half:] + carried * dots(0, 1) + second * dots(1, 1) + skips * x[1],
    ]
    scale_ref[:half] = carried
    scale_ref[half:] = second
    gain = gain_ref[...].astype(F32)
    lane = iota((half, LANES), 1)
    for token in range(2):
        gated = y[token] * silu(gates[token])
        rows = slice(token * half, (token + 1) * half)
        sent_ref[rows, :width] = (gated * gain).astype(BF16)
        squares = jnp.zeros((half, LANES), F32)
        for g in range(groups):
            part = gated[:, g * span : (g + 1) * span]
            total = jnp.sum(part * part, axis=1, keepdims=True)
            high = total.astype(BF16).astype(F32)
            squares = squares + jnp.where(lane == 2 * g, high, 0.0) + jnp.where(lane == 2 * g + 1, total - high, 0.0)
        sent_ref[rows, width:] = squares.astype(BF16)


def readout(parts, history, taps, offset, gain, read, bc, dt, head_vals, seqs, groups, chan):
    rows, width = read.shape
    heads = head_vals.shape[1]
    return pl.pallas_call(
        functools.partial(readout_kernel, parts=len(parts), seqs=seqs, groups=groups, heads=heads, chan=chan),
        out_shape=(
            jax.ShapeDtypeStruct((rows, width + LANES), BF16),
            jax.ShapeDtypeStruct((rows, width), BF16),
            jax.ShapeDtypeStruct((rows, width), F32),
            jax.ShapeDtypeStruct((rows // 2, heads), F32),
        ),
        in_specs=[VMEM_SPEC] * (len(parts) + 8),
        out_specs=(VMEM_SPEC,) * 4,
        compiler_params=params(16),
        cost_estimate=cost(100 * rows * width, 12 * rows * width),
        name="readout",
    )(*parts, history, taps, offset, gain, read, bc, dt, head_vals)


def state_write_kernel(scale_ref, decay_ref, bc_ref, state_ref, *refs, groups, first):
    new_ref, left, decays = refs[-3:]
    step = pl.program_id(0)
    count, rows, _ = state_ref.shape
    half = bc_ref.shape[0] // 2
    span = rows // groups
    heads = decay_ref.shape[1]
    chan = rows // heads
    seqs = decays.shape[0] // heads

    @pl.when(step == 0)
    def _():
        scale = scale_ref[...]
        high = scale.astype(BF16).astype(F32)
        pad = jnp.zeros((left.shape[1] - 6 * half, rows), F32)
        left[...] = jnp.concatenate([high, scale - high, high, pad], axis=0).T.astype(BF16)
        by_head = decay_ref[...].T
        for s in range(seqs):
            decays[s * heads : (s + 1) * heads] = jnp.broadcast_to(by_head[:, s : s + 1], (heads, LANES))

    row = iota((left.shape[1], STATE), 0)
    for j in range(count):
        seq = (step + first) * count + j
        for g in range(groups):
            b = [bc_ref[pl.ds(t * half + seq, 1), 2 * g * STATE : (2 * g + 1) * STATE] for t in range(2)]
            high = [value.astype(BF16).astype(F32) for value in b]
            low = [value - top for value, top in zip(b, high)]
            right = jnp.zeros(row.shape, F32)
            for block, value in enumerate(high + high + low):
                right = jnp.where(row == block * half + seq, value, right)
            here = slice(g * span, (g + 1) * span)
            added = jnp.dot(left[here], right.astype(BF16), preferred_element_type=F32)
            for h in range(span // chan):
                head = g * (span // chan) + h
                decay = decays[pl.ds(seq * heads + head, 1), :]
                decay = jnp.concatenate([decay] * (STATE // LANES), axis=1)
                new_ref[j, head * chan : (head + 1) * chan] = (
                    decay * state_ref[j, head * chan : (head + 1) * chan] + added[h * chan : (h + 1) * chan]
                )


def state_write(scale, decay, bc, state, groups, count, first, steps, before=None):
    seqs, rows, _ = state.shape
    half = bc.shape[0] // 2
    heads = decay.shape[1]
    depth = -(-6 * half // LANES) * LANES
    whole = lambda array: pl.BlockSpec(array.shape, lambda i: (0, 0))
    block = pl.BlockSpec((count, rows, STATE), lambda i: (i + first, 0, 0))
    extra = [] if before is None else [before]
    return pl.pallas_call(
        functools.partial(state_write_kernel, groups=groups, first=first),
        grid=(steps,),
        out_shape=jax.ShapeDtypeStruct(state.shape, F32),
        in_specs=[whole(scale), whole(decay), whole(bc), block] + [ANY_SPEC] * len(extra),
        out_specs=block,
        scratch_shapes=[pltpu.VMEM((rows, depth), BF16), pltpu.VMEM((seqs * heads, LANES), F32)],
        input_output_aliases={4: 0} if extra else {},
        compiler_params=params(24),
        cost_estimate=cost(4 * count * steps * rows * STATE, 8 * count * steps * rows * STATE),
        name="state_write",
    )(scale, decay, bc, state, *extra)


def out_proj_kernel(me_ref, *refs, wide, narrow, groups, group_span):
    sent = refs[:wide]
    squares = refs[wide : wide + narrow]
    w_ref = refs[wide + narrow]
    outs = refs[wide + narrow + 1 : wide + 2 * narrow + 1]
    total, chunks = refs[wide + 2 * narrow + 1 :]
    summed = squares[0][...]
    for ref in squares[1:]:
        summed = summed + ref[...]
    rows = total.shape[0]
    width = w_ref.shape[0] // wide
    span = width // groups
    lane = iota(summed.shape, 1)
    for mask in range(wide):
        owner = me_ref[0] ^ mask
        scaled = []
        for g in range(groups):
            low = (owner // group_span * group_span) * groups + g
            mine = (lane >= low) & (lane < low + (group_span - 1) * groups + 1)
            group_sum = jnp.sum(jnp.where(mine, summed, 0.0), axis=1, keepdims=True)
            inverse = lax.rsqrt(group_sum / (HEADS // NGROUPS * HEAD_DIM) + EPSILON)
            scaled.append(sent[mask][:, g * span : (g + 1) * span].astype(F32) * inverse)
        normed = jnp.concatenate(scaled, axis=1).astype(BF16)
        weight = w_ref[pl.ds(pl.multiple_of(owner * width, width), width), :]
        product = jnp.dot(normed, weight, preferred_element_type=F32)
        total[...] = product if mask == 0 else total[...] + product
    cols = total.shape[1] // narrow
    for n in range(narrow):
        chunks[n] = total[:, n * cols : (n + 1) * cols].astype(BF16)
    for mask in range(narrow):
        outs[mask][...] = chunks[me_ref[1] ^ mask]


def out_proj(me, sent, squares, weight, groups, group_span):
    wide, narrow = len(sent), len(squares)
    rows = sent[0].shape[0]
    depth, cols = weight.shape
    return pl.pallas_call(
        functools.partial(out_proj_kernel, wide=wide, narrow=narrow, groups=groups, group_span=group_span),
        out_shape=[jax.ShapeDtypeStruct((rows, cols // narrow), BF16)] * narrow,
        in_specs=[SMEM_SPEC] + [VMEM_SPEC] * (wide + narrow + 1),
        out_specs=[VMEM_SPEC] * narrow,
        scratch_shapes=[pltpu.VMEM((rows, cols), F32), pltpu.VMEM((narrow, rows, cols // narrow), BF16)],
        compiler_params=params(28),
        cost_estimate=cost(2 * rows * depth * cols, 2 * depth * cols),
        name="out_proj",
    )(me, *sent, *squares, weight)


def shards(
    inputs,
    xz_weight,
    bc_weight,
    dt_weight,
    conv_x_weight,
    conv_x_bias,
    conv_bc_weight,
    conv_bc_bias,
    conv_x_state,
    conv_bc_state,
    dt_bias,
    a_log,
    d_skip,
    norm_weight,
    out_weight,
    ssm_state,
):
    seqs = inputs.shape[0]
    feats = inputs.shape[2]
    heads = dt_weight.shape[1]
    wide = lax.axis_size("wide")
    narrow = lax.axis_size("narrow")
    chan = HEAD_DIM // narrow
    width = heads * chan
    half = -(-seqs // 8) * 8
    groups = max(NGROUPS // wide, 1)
    group_span = max(wide // NGROUPS, 1)
    depth = min(256, feats)
    me = jnp.stack([lax.axis_index("wide"), lax.axis_index("narrow")]).astype(jnp.int32)

    def rows_of(value):
        padded = jnp.pad(value, ((0, 0), (0, half - seqs), (0, 0)))
        return padded.reshape(value.shape[0] * half, value.shape[2])

    x = rows_of(inputs.transpose(1, 0, 2))
    part, spread = small_proj(x, bc_weight, dt_weight.T, depth)
    bc_parts = from_all(part, "narrow")
    chunks = big_proj(me, spread, xz_weight, depth, narrow, chan)

    conv, kept_bc, dt = bc_conv(
        bc_parts, conv_bc_state.transpose(1, 0, 2), conv_bc_weight, conv_bc_bias.reshape(1, -1)
    )
    for bit in range(group_span.bit_length() - 1):
        partner = exchanged(conv.astype(BF16), "wide", 1 << bit).astype(F32)
        is_lower = lax.axis_index("wide") // (1 << bit) % 2 == 0
        conv = jnp.where(
            is_lower, jnp.concatenate([conv, partner], axis=1), jnp.concatenate([partner, conv], axis=1)
        )

    xz_parts = [chunks[0]] + [exchanged(chunks[mask], "narrow", mask) for mask in range(1, narrow)]
    state = ssm_state.reshape(seqs, width, STATE)
    count = 2 if seqs % 2 == 0 else 1
    read = state_read(conv, state, groups, count)

    history = rows_of(conv_x_state.reshape(seqs, 3, width).transpose(1, 0, 2))
    sent, fresh, scale, decay = readout(
        xz_parts,
        history,
        conv_x_weight.reshape(-1, width),
        conv_x_bias.reshape(1, width),
        norm_weight.reshape(1, width),
        read,
        conv,
        dt,
        jnp.stack([dt_bias, a_log, d_skip]),
        seqs,
        groups,
        chan,
    )

    gathered = from_all(sent, "wide")
    steps = seqs // count
    early = steps // 2
    new_state = state_write(scale, decay, conv, state, groups, count, 0, early)
    square_parts = [value[:, width:].astype(F32) for value in gathered]
    square_parts = [
        sum(value[:, 2 * g : 2 * g + 2].sum(axis=1, keepdims=True) for value in [piece])
        for piece in square_parts
        for g in range(groups)
    ]
    wide_index = lax.axis_index("wide")
    lane = jnp.arange(LANES)[None, :]
    squares = jnp.zeros((sent.shape[0], LANES), F32)
    for mask in range(wide):
        for g in range(groups):
            place = (wide_index ^ mask) * groups + g
            squares = squares + jnp.where(lane == place, square_parts[mask * groups + g], 0.0)
    square_list = from_all(squares, "narrow")
    new_state = state_write(scale, decay, conv, state, groups, count, early, steps - early, new_state)

    out_chunks = out_proj(me, gathered, square_list, out_weight.reshape(-1, out_weight.shape[2]), groups, group_span)
    out_sum = out_chunks[0].astype(F32)
    for mask in range(1, narrow):
        out_sum = out_sum + exchanged(out_chunks[mask], "narrow", mask).astype(F32)
    layer_out = out_sum.astype(BF16).reshape(2, half, -1)[:, :seqs].transpose(1, 0, 2)

    fresh = fresh.reshape(2, half, heads, chan)[:, :seqs].transpose(1, 0, 2, 3)
    new_conv_x = jnp.concatenate([conv_x_state[:, 2:], fresh], axis=1)
    return (layer_out, new_state.reshape(ssm_state.shape), new_conv_x, kept_bc.transpose(1, 0, 2))


def solution(mesh):
    return jax.shard_map(
        shards,
        mesh=mesh,
        in_specs=(
            P("groups", None, "narrow"),
            P("narrow", None, "wide"),
            P("narrow", "wide"),
            P("narrow", "wide"),
            P(None, "wide", "narrow"),
            P("wide", "narrow"),
            P(None, "wide"),
            P("wide"),
            P("groups", None, "wide", "narrow"),
            P("groups", None, "wide"),
            P("wide"),
            P("wide"),
            P("wide"),
            P("wide", "narrow"),
            P(None, "narrow", "wide"),
            P("groups", "wide", "narrow", None),
        ),
        out_specs=(
            P("groups", None, ("wide", "narrow")),
            P("groups", "wide", "narrow", None),
            P("groups", None, "wide", "narrow"),
            P("groups", None, "wide"),
        ),
        check_vma=False,
    )
```

```python
import functools

import jax
import jax.numpy as jnp
from jax import lax
from jax.experimental import pallas as pl
from jax.experimental.pallas import tpu as pltpu
from jax.sharding import PartitionSpec as P

HEADS = 256
HEAD_DIM = 64
STATE = 256
NGROUPS = 8
LANES = 128
MIB = 2**20
PROJ_MIB = 56
NEXT_PROJ_MIB = 20
READ_MIB = 8
WRITE_MIB = 8
OUT_MIB = 36

EPSILON = 1e-05

F32 = jnp.float32
BF16 = jnp.bfloat16
VMEM_SPEC = pl.BlockSpec(memory_space=pltpu.VMEM)
SMEM_SPEC = pl.BlockSpec(memory_space=pltpu.SMEM)
ANY_SPEC = pl.BlockSpec(memory_space=pl.ANY)
HBM_SPEC = pl.BlockSpec(memory_space=pltpu.HBM)


def exchanged(value, axis, mask):
    return lax.ppermute(value, axis, [(i, i ^ mask) for i in range(lax.axis_size(axis))])


def from_all(value, axis):
    return [value] + [exchanged(value, axis, mask) for mask in range(1, lax.axis_size(axis))]


def silu(value):
    return value / (1.0 + jnp.exp(-value))


def iota(shape, dim):
    return lax.broadcasted_iota(jnp.int32, shape, dim)


def params(mib, **more):
    return pltpu.CompilerParams(vmem_limit_bytes=mib * MIB, **more)


def cost(flops, nbytes):
    return pl.CostEstimate(flops=int(flops), bytes_accessed=int(nbytes), transcendentals=0)


def spread_heads(heads, chan):
    shape = (heads, heads * chan)
    return (iota(shape, 1) // chan == iota(shape, 0)).astype(F32).astype(BF16)


def channel_lanes(refs, half, shape):
    history, taps, offset, gain = refs
    seqs, kept, chan, heads = history.shape
    values = [ref[...].reshape(-1, heads) for ref in (history, taps, offset, gain)]
    values = jnp.concatenate([value.astype(F32) for value in values], axis=0).astype(BF16)
    count = values.shape[0]
    wide = jnp.dot(values, spread_heads(heads, chan), preferred_element_type=F32)
    keep = iota(wide.shape, 0) % chan == iota(wide.shape, 1) % chan
    wide = jnp.where(keep, wide, 0.0).astype(BF16)
    given = iota((shape[0], count), 1) // chan
    target = jnp.where(given < seqs * kept, given % kept * half + given // kept, given - seqs * kept + kept * half)
    collect = (target == iota((shape[0], count), 0)).astype(F32).astype(BF16)
    return jnp.dot(collect, wide, preferred_element_type=F32).astype(BF16)


def kept_channels_kernel(history_ref, fresh_ref, out_ref):
    seqs, kept, chan, heads = history_ref.shape
    half = fresh_ref.shape[0] // 2
    shape = (2 * seqs * chan, 2 * half)
    wanted = iota(shape, 0) // chan
    wanted = wanted // seqs * half + wanted % seqs
    repeat = (wanted == iota(shape, 1)).astype(F32).astype(BF16)
    wide = jnp.dot(repeat, fresh_ref[...], preferred_element_type=F32)
    keep = iota(wide.shape, 0) % chan == iota(wide.shape, 1) % chan
    wide = jnp.where(keep, wide, 0.0).astype(BF16)
    shape = (heads * chan, heads)
    collect = (iota(shape, 0) // chan == iota(shape, 1)).astype(F32).astype(BF16)
    out = jnp.dot(wide, collect, preferred_element_type=F32)
    for seq in range(seqs):
        out_ref[seq, 0] = history_ref[seq, kept - 1]
        for token in range(2):
            row = (token * seqs + seq) * chan
            out_ref[seq, kept - 2 + token] = out[row : row + chan].astype(BF16)


def kept_channels(history, fresh):
    return pl.pallas_call(
        kept_channels_kernel,
        out_shape=jax.ShapeDtypeStruct(history.shape, BF16),
        in_specs=[VMEM_SPEC, VMEM_SPEC],
        out_specs=VMEM_SPEC,
        compiler_params=params(10),
        cost_estimate=cost(100 * fresh.size, 4 * fresh.size),
        name="kept_channels",
    )(history, fresh)


def proj_kernel(*refs, slots, first, narrow, chan, half, small):
    me_ref, w_ref = refs[:2]
    if small:
        x_ref, bc_ref, dt_ref, spread, mover = refs[2:7]
        x_held, bc_held, dt_held, x_sem, bc_sem, dt_sem = refs[-6:]
        refs = refs[7:-6]
    else:
        spread, mover = refs[2:4]
        channel_refs = refs[4:8]
        later_ref, later, lanes_ref = refs[8:11]
        later_sem = refs[-1]
        refs = refs[11:-1]
    outs = refs[:narrow]
    held, flat, total, chunks, held_sem, flat_sem = refs[narrow:]
    feats = w_ref.shape[0]
    rows = spread.shape[0] // 2
    span = mover.shape[0]
    pair = held.shape[1]
    blocks = total.shape[1] // LANES
    steps = blocks // pair

    def copies(i):
        return [
            pltpu.make_async_copy(
                w_ref.at[:, first + i * pair + j], held.at[i % slots, j], held_sem.at[i % slots, j]
            )
            for j in range(pair)
        ]

    def flat_copy(i):
        source = held.at[i % slots].reshape(pair * 2 * feats, LANES)
        return pltpu.make_async_copy(source, flat.at[i % 2], flat_sem.at[i % 2])

    parts = 0 if small else later.shape[0]

    def later_copy(i):
        return pltpu.make_async_copy(later_ref.at[i], later.at[i], later_sem.at[i])

    if small:
        x_copy = pltpu.make_async_copy(x_ref, x_held, x_sem)
        bc_copy = pltpu.make_async_copy(bc_ref, bc_held, bc_sem)
        dt_copy = pltpu.make_async_copy(dt_ref, dt_held, dt_sem)
        x_copy.start()
    for i in range(min(slots, steps)):
        for copy in copies(i):
            copy.start()
    if small:
        bc_copy.start()
        dt_copy.start()

    if small:
        x_copy.wait()
        seqs, tokens, _ = x_held.shape
        given = iota((rows, tokens * seqs), 1)
        wanted = iota((rows, tokens * seqs), 0)
        order = (given % tokens * half + given // tokens == wanted).astype(F32).astype(BF16)
        x = jnp.dot(order, x_held[...].reshape(tokens * seqs, feats), preferred_element_type=F32)
        x = x.astype(BF16)
        piece = min(256, feats)
        pieces = feats // piece
        stacked = jnp.concatenate([x[:, i * piece : (i + 1) * piece] for i in range(pieces)], axis=0)
        place = iota((piece, 2 * piece), 1) - 2 * iota((piece, 2 * piece), 0)
        for z in range(2):
            one_hot = (place == z).astype(F32).astype(BF16)
            moved = jnp.dot(stacked, one_hot, preferred_element_type=F32).astype(BF16)
            for i in range(pieces):
                columns = slice(2 * i * piece, 2 * (i + 1) * piece)
                spread[z * rows : (z + 1) * rows, columns] = moved[i * rows : (i + 1) * rows]
        column = iota((span, span), 0)
        target = (column % HEAD_DIM) // chan * (span // narrow) + column // HEAD_DIM * chan + column % chan
        mover[...] = (target == iota((span, span), 1)).astype(F32).astype(BF16)

    else:
        lanes_ref[...] = channel_lanes(channel_refs, half, lanes_ref.shape)

    def arrived(i):
        for copy in copies(i):
            copy.wait()
        flat_copy(i).start()

    arrived(0)
    for i in range(steps):
        flat_copy(i).wait()
        if i + slots < steps:
            for copy in copies(i + slots):
                copy.start()
        for j in range(i * parts // steps, (i + 1) * parts // steps):
            later_copy(j).start()
        if i + 1 < steps:
            arrived(i + 1)
        weight = jnp.concatenate([flat[i % 2, j * 2 * feats : (j + 1) * 2 * feats] for j in range(pair)], axis=1)
        columns = slice(i * pair * LANES, (i + 1) * pair * LANES)
        total[:, columns] = jnp.dot(spread[...], weight, preferred_element_type=F32).astype(BF16)
        if (i + 1) * pair * LANES % span == 0:
            q = (i + 1) * pair * LANES // span - 1
            part = span // narrow
            moved = jnp.dot(total[:, q * span : (q + 1) * span], mover[...], preferred_element_type=F32)
            for n in range(narrow):
                chunks[n, :, q * part : (q + 1) * part] = moved[:, n * part : (n + 1) * part].astype(BF16)
    if small:
        bc_copy.wait()
        dt_copy.wait()
        bc_part = jnp.dot(x, bc_held[...], preferred_element_type=F32)
        dt_part = lax.dot_general(x, dt_held[...], (((1,), (1,)), ((), ())), preferred_element_type=F32)
        chunk_cols, cols = chunks.shape[2], outs[0].shape[1]
        pad = jnp.zeros((rows, 2 * (cols - chunk_cols) - bc_part.shape[1] - dt_part.shape[1]), F32)
        sums = jnp.concatenate([bc_part, dt_part, pad], axis=1).astype(BF16)
        for mask in range(narrow):
            outs[mask][:rows, chunk_cols:] = sums[:, : cols - chunk_cols]
            outs[mask][rows:, chunk_cols:] = sums[:, cols - chunk_cols :]
    for mask in range(narrow):
        outs[mask][:, : chunks.shape[2]] = chunks[me_ref[1] ^ mask]
    for j in range(parts):
        later_copy(j).wait()


def proj(me, weight, given, half, narrow, chan, first, blocks, small, slots=4):
    feats, _, cols = weight.shape
    rows = 2 * half
    pair = 2 if blocks % 2 == 0 else 1
    by_block = weight.reshape(feats, 2, cols // LANES, LANES).transpose(0, 2, 1, 3)
    cols = blocks * LANES // narrow
    scratch = [
        pltpu.VMEM((slots, pair, feats, 2, LANES), BF16),
        pltpu.VMEM((2, pair * 2 * feats, LANES), BF16),
        pltpu.VMEM((2 * rows, blocks * LANES), BF16),
        pltpu.VMEM((narrow, 2 * rows, blocks * LANES // narrow), BF16),
        pltpu.SemaphoreType.DMA((slots, pair)),
        pltpu.SemaphoreType.DMA((2,)),
    ]
    specs = [VMEM_SPEC] * len(given)
    nbytes = 4 * feats * blocks * LANES
    if small:
        inputs, bc_weight, dt_weight_t = given
        span = min(narrow, blocks) * LANES
        out_shape = [
            jax.ShapeDtypeStruct((2 * rows, 2 * feats), BF16),
            jax.ShapeDtypeStruct((span, span), BF16),
        ]
        cols += -(-(bc_weight.shape[1] + dt_weight_t.shape[0]) // (2 * LANES)) * LANES
        scratch += [pltpu.VMEM(value.shape, BF16) for value in given] + [pltpu.SemaphoreType.DMA] * 3
        specs = [HBM_SPEC] * 3
        nbytes += 2 * (bc_weight.size + dt_weight_t.size)
    else:
        history, later = given[2], given[-1]
        specs[-1] = HBM_SPEC
        nbytes += later.size * later.dtype.itemsize
        scratch += [pltpu.SemaphoreType.DMA((later.shape[0],))]
        out_shape = [jax.ShapeDtypeStruct(later.shape, later.dtype)]
        out_shape += [jax.ShapeDtypeStruct((3 * half + 8, history.shape[2] * history.shape[3]), BF16)]
    out_shape += [jax.ShapeDtypeStruct((2 * rows, cols), BF16)] * narrow
    return pl.pallas_call(
        functools.partial(
            proj_kernel, slots=slots, first=first, narrow=narrow, chan=chan, half=half, small=small
        ),
        out_shape=out_shape,
        in_specs=[SMEM_SPEC, HBM_SPEC] + specs,
        out_specs=[VMEM_SPEC] * len(out_shape),
        scratch_shapes=scratch,
        compiler_params=params(PROJ_MIB if small else NEXT_PROJ_MIB),
        cost_estimate=cost(rows * nbytes, nbytes),
        name="proj_small" if small else "proj",
    )(me, by_block, *given)


def conv_pair(history, fresh, taps, offset):
    window = list(history) + list(fresh)
    outputs = []
    for token in range(2):
        summed = offset
        for tap in range(4):
            summed = summed + taps[tap : tap + 1] * window[token + tap]
        outputs.append(silu(summed))
    return outputs


def summed_refs(refs):
    total = refs[0][...].astype(F32)
    for ref in refs[1:]:
        total = total + ref[...].astype(F32)
    return total


def bc_conv_kernel(*refs, parts, seqs):
    history_ref, taps_ref, offset_ref, conv_ref, kept_ref, dt_ref, chan_ref = refs[parts:]
    rows, chunk_cols = conv_ref.shape[0], chan_ref.shape[1]
    both = summed_refs(refs[:parts])
    chan_ref[...] = both[:, :chunk_cols].astype(BF16)
    summed = jnp.concatenate([both[:rows, chunk_cols:], both[rows:, chunk_cols:]], axis=1)
    half = summed.shape[0] // 2
    cols = taps_ref.shape[1]
    proj = summed.astype(BF16).astype(F32)
    dt_ref[...] = proj[:, cols : cols + LANES]
    fresh = [proj[:seqs, :cols], proj[half : half + seqs, :cols]]
    history = [history_ref[i].astype(F32) for i in range(3)]
    conv_ref[...] = jnp.zeros_like(conv_ref)
    for token, value in enumerate(conv_pair(history, fresh, taps_ref[...].astype(F32), offset_ref[...].astype(F32))):
        conv_ref[token * half : token * half + seqs] = value
    kept_ref[0] = history_ref[2]
    kept_ref[1] = fresh[0].astype(BF16)
    kept_ref[2] = fresh[1].astype(BF16)


def bc_conv(parts, history, taps, offset, chunk_cols):
    rows = parts[0].shape[0]
    cols = taps.shape[1]
    return pl.pallas_call(
        functools.partial(bc_conv_kernel, parts=len(parts), seqs=history.shape[1]),
        out_shape=(
            jax.ShapeDtypeStruct((rows // 2, cols), F32),
            jax.ShapeDtypeStruct(history.shape, BF16),
            jax.ShapeDtypeStruct((rows // 2, LANES), F32),
            jax.ShapeDtypeStruct((rows, chunk_cols), BF16),
        ),
        in_specs=[VMEM_SPEC] * (len(parts) + 3),
        out_specs=(VMEM_SPEC,) * 4,
        compiler_params=params(8),
        cost_estimate=cost(30 * rows * cols, 8 * rows * cols),
        name="bc_conv",
    )(*parts, history, taps, offset)


def state_read_kernel(bc_ref, state_ref, read_ref, *, groups):
    seqs, rows, _ = state_ref.shape
    half = bc_ref.shape[0] // 2
    span = rows // groups
    read_ref[...] = jnp.zeros_like(read_ref)
    for seq in range(seqs):
        for g in range(groups):
            cols = slice((2 * g + 1) * STATE, (2 * g + 2) * STATE)
            both = jnp.concatenate([bc_ref[t * half + seq : t * half + seq + 1, cols] for t in range(2)], axis=0)
            held = state_ref[seq, g * span : (g + 1) * span].astype(BF16)
            out = lax.dot_general(both.astype(BF16), held, (((1,), (1,)), ((), ())), preferred_element_type=F32)
            for t in range(2):
                read_ref[t * half + seq : t * half + seq + 1, g * span : (g + 1) * span] = out[t : t + 1]


def state_read(bc, state, groups):
    seqs, rows, _ = state.shape
    return pl.pallas_call(
        functools.partial(state_read_kernel, groups=groups),
        out_shape=jax.ShapeDtypeStruct((bc.shape[0], rows), F32),
        in_specs=[VMEM_SPEC, VMEM_SPEC],
        out_specs=VMEM_SPEC,
        compiler_params=params(READ_MIB),
        cost_estimate=cost(4 * state.size, 4 * state.size),
        name="state_read",
    )(bc, state)


def readout_kernel(*refs, parts, groups, heads, chan):
    done_ref, part_refs = refs[0], refs[1 : parts + 1]
    lanes_ref, read_ref, bc_ref, dt_ref, heads_ref = refs[parts + 1 : parts + 6]
    sent_ref, fresh_ref, scale_ref, decay_ref = refs[parts + 6 :]
    columns = [done_ref[...].astype(F32)]
    if part_refs:
        columns.append(summed_refs(part_refs).astype(BF16).astype(F32))
    proj = jnp.concatenate(columns, axis=1)
    half = proj.shape[0] // 4
    width = proj.shape[1]
    gates = [proj[:half], proj[half : 2 * half]]
    fresh = [proj[2 * half : 3 * half], proj[3 * half :]]
    fresh_ref[...] = proj[2 * half :].astype(BF16)
    lanes = lanes_ref[...].astype(F32)
    history = [lanes[i * half : (i + 1) * half] for i in range(3)]
    taps, offset, gain = (lanes[3 * half + i : 3 * half + j] for i, j in ((0, 4), (4, 5), (5, 6)))
    x = conv_pair(history, fresh, taps, offset)

    bias, rate, skip = heads_ref[0:1], jnp.exp(heads_ref[1:2]), heads_ref[2:3]
    raw = dt_ref[:, :heads] + bias
    step = jnp.maximum(raw, 0.0) + jnp.log1p(jnp.exp(-jnp.abs(raw)))
    decay = jnp.exp(-step * rate)
    decay_ref[...] = decay[:half] * decay[half:]
    repeat = (iota((heads, width), 1) // chan == iota((heads, width), 0)).astype(F32)
    packed = jnp.concatenate([step, decay, jnp.broadcast_to(skip, (8, heads))], axis=0)
    spread = jnp.dot(packed, repeat, preferred_element_type=F32, precision=lax.Precision.HIGHEST)
    steps = [spread[:half], spread[half : 2 * half]]
    decays = [spread[2 * half : 3 * half], spread[3 * half : 4 * half]]
    skips = spread[4 * half : 4 * half + 1]

    span = width // groups

    def dots(b_token, c_token):
        out = []
        for g in range(groups):
            b = bc_ref[b_token * half : (b_token + 1) * half, 2 * g * STATE : (2 * g + 1) * STATE]
            c = bc_ref[c_token * half : (c_token + 1) * half, (2 * g + 1) * STATE : (2 * g + 2) * STATE]
            out.append(jnp.broadcast_to(jnp.sum(b * c, axis=1, keepdims=True), (half, span)))
        return jnp.concatenate(out, axis=1)

    first = steps[0] * x[0]
    second = steps[1] * x[1]
    carried = decays[1] * first
    y = [
        decays[0] * read_ref[:half] + first * dots(0, 0) + skips * x[0],
        decays[0] * decays[1] * read_ref[half:] + carried * dots(0, 1) + second * dots(1, 1) + skips * x[1],
    ]
    scale_ref[:half] = carried
    scale_ref[half:] = second
    lane = iota((half, LANES), 1)
    for token in range(2):
        gated = y[token] * silu(gates[token])
        rows = slice(token * half, (token + 1) * half)
        sent_ref[rows, :width] = (gated * gain).astype(BF16)
        squares = jnp.zeros((half, LANES), F32)
        for g in range(groups):
            part = gated[:, g * span : (g + 1) * span]
            total = jnp.sum(part * part, axis=1, keepdims=True)
            high = total.astype(BF16).astype(F32)
            squares = squares + jnp.where(lane == 2 * g, high, 0.0) + jnp.where(lane == 2 * g + 1, total - high, 0.0)
        sent_ref[rows, width:] = squares.astype(BF16)


def readout(done, parts, lanes, read, bc, dt, head_vals, groups, chan):
    rows, width = read.shape
    heads = head_vals.shape[1]
    return pl.pallas_call(
        functools.partial(readout_kernel, parts=len(parts), groups=groups, heads=heads, chan=chan),
        out_shape=(
            jax.ShapeDtypeStruct((rows, width + LANES), BF16),
            jax.ShapeDtypeStruct((rows, width), BF16),
            jax.ShapeDtypeStruct((rows, width), F32),
            jax.ShapeDtypeStruct((rows // 2, heads), F32),
        ),
        in_specs=[VMEM_SPEC] * (len(parts) + 6),
        out_specs=(VMEM_SPEC,) * 4,
        compiler_params=params(16),
        cost_estimate=cost(100 * rows * width, 12 * rows * width),
        name="readout",
    )(done, *parts, lanes, read, bc, dt, head_vals)


def state_write_kernel(*refs, groups, heads, first, count, prepare):
    if prepare:
        scale_ref, decay_ref, bc_ref, state_ref, new_ref, left, decays = refs[:7]
        refs = refs[7:]
    else:
        left, decays, bc_ref, state_ref, _, _, new_ref, mark_ref = refs[:8]
        refs = refs[8:]
        mark_ref[...] = jnp.zeros_like(mark_ref)
    right, made, sems = refs
    seqs, rows, _ = state_ref.shape
    half = bc_ref.shape[0] // 2
    span = rows // groups
    chan = rows // heads
    slots = made.shape[0]
    right[...] = jnp.zeros_like(right)
    if prepare:
        scale = scale_ref[...]
        high = scale.astype(BF16).astype(F32)
        pad = jnp.zeros((left.shape[1] - 6 * half, rows), F32)
        left[...] = jnp.concatenate([high, scale - high, high, pad], axis=0).T.astype(BF16)
        by_head = decay_ref[...].T
        for s in range(seqs):
            decays[s * heads : (s + 1) * heads] = jnp.broadcast_to(by_head[:, s : s + 1], (heads, LANES))

    def out_copy(seq):
        slot = (seq - first) % slots
        return pltpu.make_async_copy(made.at[slot], new_ref.at[seq], sems.at[slot])

    for seq in range(first, first + count):
        slot = (seq - first) % slots
        side = (seq - first) % right.shape[0]
        values = []
        for t in range(2):
            row = bc_ref[t * half + seq : t * half + seq + 1, :]
            values.append(jnp.concatenate([row[:, 2 * g * STATE : (2 * g + 1) * STATE] for g in range(groups)], axis=1))
        high = [value.astype(BF16).astype(F32) for value in values]
        low = [value - top for value, top in zip(values, high)]
        for block, value in enumerate(high + high + low):
            right[side, block * half + seq : block * half + seq + 1, :] = value
        if seq - first >= slots:
            out_copy(seq - slots).wait()
        for g in range(groups):
            here = slice(g * span, (g + 1) * span)
            factor = right[side, :, g * STATE : (g + 1) * STATE].astype(BF16)
            added = jnp.dot(left[here], factor, preferred_element_type=F32)
            for h in range(span // chan):
                head = g * (span // chan) + h
                decay = decays[seq * heads + head : seq * heads + head + 1, :]
                decay = jnp.concatenate([decay] * (STATE // LANES), axis=1)
                made[slot, head * chan : (head + 1) * chan] = (
                    decay * state_ref[seq, head * chan : (head + 1) * chan] + added[h * chan : (h + 1) * chan]
                )
        out_copy(seq).start()
        for block in range(6):
            right[side, block * half + seq : block * half + seq + 1, :] = jnp.zeros((1, right.shape[2]), F32)
    for seq in range(max(first, first + count - slots), first + count):
        out_copy(seq).wait()


def state_write(given, bc, state, groups, heads, first, count, before=None, after=None):
    seqs, rows, _ = state.shape
    half = bc.shape[0] // 2
    prepare = before is None
    depth = -(-6 * half // LANES) * LANES
    scratch = [
        pltpu.VMEM((2, depth, groups * STATE), F32),
        pltpu.VMEM((3, rows, STATE), F32),
        pltpu.SemaphoreType.DMA((3,)),
    ]
    if prepare:
        more = [
            jax.ShapeDtypeStruct((rows, depth), BF16),
            jax.ShapeDtypeStruct((seqs * heads, LANES), F32),
        ]
        extra = []
    else:
        more = [jax.ShapeDtypeStruct((8, LANES), F32)]
        extra = [before, after]
    nbytes = 4 * count * rows * STATE
    return pl.pallas_call(
        functools.partial(
            state_write_kernel, groups=groups, heads=heads, first=first, count=count, prepare=prepare
        ),
        out_shape=[jax.ShapeDtypeStruct(state.shape, F32)] + more,
        in_specs=[VMEM_SPEC] * 4 + [HBM_SPEC] * len(extra),
        out_specs=[HBM_SPEC] + [VMEM_SPEC] * len(more),
        scratch_shapes=scratch,
        input_output_aliases={} if prepare else {4: 0},
        compiler_params=params(WRITE_MIB),
        cost_estimate=cost(nbytes, 2 * nbytes),
        name="state_write",
    )(*given, bc, state, *extra)


def squares_kernel(me_ref, *refs, wide, groups):
    sent, out_ref = refs[:wide], refs[-1]
    rows, lanes = out_ref.shape
    lane = iota((rows, lanes), 1)
    total = jnp.zeros((rows, lanes), F32)
    for mask in range(wide):
        owner = me_ref[0] ^ mask
        value = sent[mask][:, sent[mask].shape[1] - lanes :].astype(F32)
        for g in range(groups):
            own = value[:, 2 * g : 2 * g + 1] + value[:, 2 * g + 1 : 2 * g + 2]
            total = total + jnp.where(lane == owner * groups + g, own, 0.0)
    out_ref[...] = total


def all_squares(me, sent, groups, after):
    wide = len(sent)
    return pl.pallas_call(
        functools.partial(squares_kernel, wide=wide, groups=groups),
        out_shape=jax.ShapeDtypeStruct((sent[0].shape[0], LANES), F32),
        in_specs=[SMEM_SPEC] + [VMEM_SPEC] * wide + [ANY_SPEC],
        out_specs=VMEM_SPEC,
        compiler_params=params(8),
        cost_estimate=cost(LANES * LANES * wide, 4 * LANES * LANES * wide),
        name="all_squares",
    )(me, *sent, after)


def out_proj_kernel(me_ref, *refs, wide, groups):
    sent = refs[:wide]
    w_ref, _, made_ref, held, sems = refs[wide:]
    width = w_ref.shape[0] // wide
    span = width // groups

    def copy(mask):
        owner = me_ref[0] ^ mask
        rows = pl.ds(pl.multiple_of(owner * width, width), width)
        return pltpu.make_async_copy(w_ref.at[rows], held.at[mask], sems.at[mask])

    for mask in range(wide):
        copy(mask).start()
    for mask in range(wide):
        copy(mask).wait()
        for g in range(groups):
            rows = slice(g * span, (g + 1) * span)
            product = jnp.dot(sent[mask][:, rows], held[mask, rows], preferred_element_type=F32)
            made_ref[mask * groups + g] = product


def out_proj(me, sent, weight, groups, after):
    wide = len(sent)
    rows = sent[0].shape[0]
    depth, cols = weight.shape
    return pl.pallas_call(
        functools.partial(out_proj_kernel, wide=wide, groups=groups),
        out_shape=jax.ShapeDtypeStruct((wide * groups, rows, cols), F32),
        in_specs=[SMEM_SPEC] + [VMEM_SPEC] * wide + [HBM_SPEC, ANY_SPEC],
        out_specs=VMEM_SPEC,
        scratch_shapes=[pltpu.VMEM((wide, depth // wide, cols), BF16), pltpu.SemaphoreType.DMA((wide,))],
        compiler_params=params(OUT_MIB),
        cost_estimate=cost(2 * rows * depth * cols, 2 * depth * cols),
        name="out_proj",
    )(me, *sent, weight, after)


def out_scale_kernel(me_ref, made_ref, *refs, wide, narrow, groups, group_span):
    squares, outs, chunks = refs[:narrow], refs[narrow : 2 * narrow], refs[-1]
    summed = summed_refs(squares)
    lane = iota(summed.shape, 1)
    total = None
    for mask in range(wide):
        owner = me_ref[0] ^ mask
        for g in range(groups):
            low = (owner // group_span * group_span) * groups + g
            mine = (lane >= low) & (lane < low + (group_span - 1) * groups + 1)
            group_sum = jnp.sum(jnp.where(mine, summed, 0.0), axis=1, keepdims=True)
            inverse = lax.rsqrt(group_sum / (HEADS // NGROUPS * HEAD_DIM) + EPSILON)
            scaled = made_ref[mask * groups + g] * inverse
            total = scaled if total is None else total + scaled
    cols = total.shape[1] // narrow
    for n in range(narrow):
        chunks[n] = total[:, n * cols : (n + 1) * cols].astype(BF16)
    for mask in range(narrow):
        outs[mask][...] = chunks[me_ref[1] ^ mask]


def out_scale(me, made, squares, wide, groups, group_span):
    narrow = len(squares)
    _, rows, cols = made.shape
    return pl.pallas_call(
        functools.partial(out_scale_kernel, wide=wide, narrow=narrow, groups=groups, group_span=group_span),
        out_shape=[jax.ShapeDtypeStruct((rows, cols // narrow), BF16)] * narrow,
        in_specs=[SMEM_SPEC] + [VMEM_SPEC] * (narrow + 1),
        out_specs=[VMEM_SPEC] * narrow,
        scratch_shapes=[pltpu.VMEM((narrow, rows, cols // narrow), BF16)],
        compiler_params=params(8),
        cost_estimate=cost(4 * made.size, 4 * made.size),
        name="out_scale",
    )(me, made, *squares)


def shards(
    inputs,
    xz_weight,
    bc_weight,
    dt_weight,
    conv_x_weight,
    conv_x_bias,
    conv_bc_weight,
    conv_bc_bias,
    conv_x_state,
    conv_bc_state,
    dt_bias,
    a_log,
    d_skip,
    norm_weight,
    out_weight,
    ssm_state,
):
    seqs = inputs.shape[0]
    feats = inputs.shape[2]
    heads = dt_weight.shape[1]
    wide = lax.axis_size("wide")
    narrow = lax.axis_size("narrow")
    chan = HEAD_DIM // narrow
    width = heads * chan
    half = -(-seqs // 8) * 8
    groups = max(NGROUPS // wide, 1)
    group_span = max(wide // NGROUPS, 1)
    me = jnp.stack([lax.axis_index("wide"), lax.axis_index("narrow")]).astype(jnp.int32)

    blocks = xz_weight.shape[2] // LANES
    cut = blocks // 2
    state = ssm_state.reshape(seqs, width, STATE)
    given = (inputs, bc_weight, dt_weight.T)
    spread, mover, *chunks = proj(me, xz_weight, given, half, narrow, chan, 0, cut, True)
    early_parts = [chunks[0]] + [exchanged(chunks[mask], "narrow", mask) for mask in range(1, narrow)]
    history = conv_x_state.transpose(0, 1, 3, 2)
    given = (spread, mover, history, conv_x_weight.transpose(0, 2, 1), conv_x_bias.T, norm_weight.T, state)
    state, lanes, *chunks = proj(me, xz_weight, given, half, narrow, chan, cut, blocks - cut, False)
    late_parts = [chunks[0]] + [exchanged(chunks[mask], "narrow", mask) for mask in range(1, narrow)]

    conv, kept_bc, dt, early_done = bc_conv(
        early_parts, conv_bc_state.transpose(1, 0, 2), conv_bc_weight, conv_bc_bias.reshape(1, -1), chunks[0].shape[1]
    )
    for bit in range(group_span.bit_length() - 1):
        partner = exchanged(conv.astype(BF16), "wide", 1 << bit).astype(F32)
        is_lower = lax.axis_index("wide") // (1 << bit) % 2 == 0
        conv = jnp.where(
            is_lower, jnp.concatenate([conv, partner], axis=1), jnp.concatenate([partner, conv], axis=1)
        )

    read = state_read(conv, state, groups)

    sent, fresh, scale, decay = readout(
        early_done,
        late_parts,
        lanes,
        read,
        conv,
        dt,
        jnp.stack([dt_bias, a_log, d_skip]),
        groups,
        chan,
    )

    gathered = from_all(sent, "wide")
    early = seqs * 3 // 5
    new_state, left, decays = state_write((scale, decay), conv, state, groups, heads, 0, early)
    squares = all_squares(me, gathered, groups, left)
    square_list = from_all(squares, "narrow")
    made = out_proj(me, gathered, out_weight.reshape(-1, out_weight.shape[2]), groups, squares)
    out_chunks = out_scale(me, made, square_list, wide, groups, group_span)
    new_state, _ = state_write(
        (left, decays), conv, state, groups, heads, early, seqs - early, new_state, out_chunks[0]
    )
    out_sum = out_chunks[0].astype(F32)
    for mask in range(1, narrow):
        out_sum = out_sum + exchanged(out_chunks[mask], "narrow", mask).astype(F32)
    layer_out = out_sum.astype(BF16).reshape(2, half, -1)[:, :seqs].transpose(1, 0, 2)

    new_conv_x = kept_channels(history, fresh).transpose(0, 1, 3, 2)
    return (layer_out, new_state.reshape(ssm_state.shape), new_conv_x, kept_bc.transpose(1, 0, 2))


def solution(mesh):
    return jax.shard_map(
        shards,
        mesh=mesh,
        in_specs=(
            P("groups", None, "narrow"),
            P("narrow", None, "wide"),
            P("narrow", "wide"),
            P("narrow", "wide"),
            P(None, "wide", "narrow"),
            P("wide", "narrow"),
            P(None, "wide"),
            P("wide"),
            P("groups", None, "wide", "narrow"),
            P("groups", None, "wide"),
            P("wide"),
            P("wide"),
            P("wide"),
            P("wide", "narrow"),
            P(None, "narrow", "wide"),
            P("groups", "wide", "narrow", None),
        ),
        out_specs=(
            P("groups", None, ("wide", "narrow")),
            P("groups", "wide", "narrow", None),
            P("groups", None, "wide", "narrow"),
            P("groups", None, "wide"),
        ),
        check_vma=False,
    )
```

```python
import functools

import jax
import jax.numpy as jnp
from jax import lax
from jax.experimental import pallas as pl
from jax.experimental.pallas import tpu as pltpu
from jax.sharding import PartitionSpec as P

HEADS = 256
HEAD_DIM = 64
STATE = 256
NGROUPS = 8
LANES = 128
MIB = 2**20
PROJ_MIB = 56
NEXT_PROJ_MIB = 20
READ_MIB = 8
WRITE_MIB = 8
OUT_MIB = 36

EPSILON = 1e-05

F32 = jnp.float32
BF16 = jnp.bfloat16
VMEM_SPEC = pl.BlockSpec(memory_space=pltpu.VMEM)
SMEM_SPEC = pl.BlockSpec(memory_space=pltpu.SMEM)
ANY_SPEC = pl.BlockSpec(memory_space=pl.ANY)
HBM_SPEC = pl.BlockSpec(memory_space=pltpu.HBM)


def exchanged(value, axis, mask):
    return lax.ppermute(value, axis, [(i, i ^ mask) for i in range(lax.axis_size(axis))])


def from_all(value, axis):
    return [value] + [exchanged(value, axis, mask) for mask in range(1, lax.axis_size(axis))]


def silu(value):
    return value / (1.0 + jnp.exp(-value))


def iota(shape, dim):
    return lax.broadcasted_iota(jnp.int32, shape, dim)


def params(mib, **more):
    return pltpu.CompilerParams(vmem_limit_bytes=mib * MIB, **more)


def cost(flops, nbytes):
    return pl.CostEstimate(flops=int(flops), bytes_accessed=int(nbytes), transcendentals=0)


def spread_heads(heads, chan):
    shape = (heads, heads * chan)
    return (iota(shape, 1) // chan == iota(shape, 0)).astype(F32).astype(BF16)


def channel_lanes(refs, half, shape):
    history, taps, offset, gain = refs
    seqs, kept, chan, heads = history.shape
    values = [ref[...].reshape(-1, heads) for ref in (history, taps, offset, gain)]
    values = jnp.concatenate([value.astype(F32) for value in values], axis=0).astype(BF16)
    count = values.shape[0]
    wide = jnp.dot(values, spread_heads(heads, chan), preferred_element_type=F32)
    keep = iota(wide.shape, 0) % chan == iota(wide.shape, 1) % chan
    wide = jnp.where(keep, wide, 0.0).astype(BF16)
    given = iota((shape[0], count), 1) // chan
    target = jnp.where(given < seqs * kept, given % kept * half + given // kept, given - seqs * kept + kept * half)
    collect = (target == iota((shape[0], count), 0)).astype(F32).astype(BF16)
    return jnp.dot(collect, wide, preferred_element_type=F32).astype(BF16)


def kept_channels_kernel(history_ref, fresh_ref, out_ref):
    seqs, kept, chan, heads = history_ref.shape
    half = fresh_ref.shape[0] // 2
    shape = (2 * seqs * chan, 2 * half)
    wanted = iota(shape, 0) // chan
    wanted = wanted // seqs * half + wanted % seqs
    repeat = (wanted == iota(shape, 1)).astype(F32).astype(BF16)
    wide = jnp.dot(repeat, fresh_ref[...], preferred_element_type=F32)
    keep = iota(wide.shape, 0) % chan == iota(wide.shape, 1) % chan
    wide = jnp.where(keep, wide, 0.0).astype(BF16)
    shape = (heads * chan, heads)
    collect = (iota(shape, 0) // chan == iota(shape, 1)).astype(F32).astype(BF16)
    out = jnp.dot(wide, collect, preferred_element_type=F32)
    for seq in range(seqs):
        out_ref[seq, 0] = history_ref[seq, kept - 1]
        for token in range(2):
            row = (token * seqs + seq) * chan
            out_ref[seq, kept - 2 + token] = out[row : row + chan].astype(BF16)


def kept_channels(history, fresh):
    return pl.pallas_call(
        kept_channels_kernel,
        out_shape=jax.ShapeDtypeStruct(history.shape, BF16),
        in_specs=[VMEM_SPEC, VMEM_SPEC],
        out_specs=VMEM_SPEC,
        compiler_params=params(10),
        cost_estimate=cost(100 * fresh.size, 4 * fresh.size),
        name="kept_channels",
    )(history, fresh)


def proj_kernel(*refs, slots, first, narrow, chan, half, small):
    me_ref, w_ref, x_ref = refs[:3]
    if small:
        bc_ref, dt_ref = refs[3:5]
        bc_held, dt_held, bc_sem, dt_sem = refs[-4:]
        refs = refs[5:-4]
    else:
        channel_refs = refs[3:7]
        later_ref, later, lanes_ref = refs[7:10]
        later_sem = refs[-1]
        refs = refs[10:-1]
    outs = refs[:narrow]
    held, flat, x_held, spread, mover, total, chunks, held_sem, flat_sem, x_sem = refs[narrow:]
    feats = w_ref.shape[0]
    rows = spread.shape[0] // 2
    span = mover.shape[0]
    pair = held.shape[1]
    blocks = total.shape[1] // LANES
    steps = blocks // pair

    def copies(i):
        return [
            pltpu.make_async_copy(
                w_ref.at[:, first + i * pair + j], held.at[i % slots, j], held_sem.at[i % slots, j]
            )
            for j in range(pair)
        ]

    def flat_copy(i):
        source = held.at[i % slots].reshape(pair * 2 * feats, LANES)
        return pltpu.make_async_copy(source, flat.at[i % 2], flat_sem.at[i % 2])

    parts = 0 if small else later.shape[0]

    def later_copy(i):
        return pltpu.make_async_copy(later_ref.at[i], later.at[i], later_sem.at[i])

    x_copy = pltpu.make_async_copy(x_ref, x_held, x_sem)
    x_copy.start()
    if small:
        bc_copy = pltpu.make_async_copy(bc_ref, bc_held, bc_sem)
        dt_copy = pltpu.make_async_copy(dt_ref, dt_held, dt_sem)
    for i in range(min(slots, steps)):
        for copy in copies(i):
            copy.start()
    if small:
        bc_copy.start()
        dt_copy.start()

    x_copy.wait()
    seqs, tokens, _ = x_held.shape
    given = iota((rows, tokens * seqs), 1)
    wanted = iota((rows, tokens * seqs), 0)
    order = (given % tokens * half + given // tokens == wanted).astype(F32).astype(BF16)
    x = jnp.dot(order, x_held[...].reshape(tokens * seqs, feats), preferred_element_type=F32)
    x = x.astype(BF16)
    piece = min(256, feats)
    pieces = feats // piece
    stacked = jnp.concatenate([x[:, i * piece : (i + 1) * piece] for i in range(pieces)], axis=0)
    place = iota((piece, 2 * piece), 1) - 2 * iota((piece, 2 * piece), 0)
    for z in range(2):
        one_hot = (place == z).astype(F32).astype(BF16)
        moved = jnp.dot(stacked, one_hot, preferred_element_type=F32).astype(BF16)
        for i in range(pieces):
            columns = slice(2 * i * piece, 2 * (i + 1) * piece)
            spread[z * rows : (z + 1) * rows, columns] = moved[i * rows : (i + 1) * rows]
    column = iota((span, span), 0)
    target = (column % HEAD_DIM) // chan * (span // narrow) + column // HEAD_DIM * chan + column % chan
    mover[...] = (target == iota((span, span), 1)).astype(F32).astype(BF16)
    if not small:
        lanes_ref[...] = channel_lanes(channel_refs, half, lanes_ref.shape)

    def arrived(i):
        for copy in copies(i):
            copy.wait()
        flat_copy(i).start()

    arrived(0)
    for i in range(steps):
        flat_copy(i).wait()
        if i + slots < steps:
            for copy in copies(i + slots):
                copy.start()
        for j in range(i * parts // steps, (i + 1) * parts // steps):
            later_copy(j).start()
        if i + 1 < steps:
            arrived(i + 1)
        weight = jnp.concatenate([flat[i % 2, j * 2 * feats : (j + 1) * 2 * feats] for j in range(pair)], axis=1)
        columns = slice(i * pair * LANES, (i + 1) * pair * LANES)
        total[:, columns] = jnp.dot(spread[...], weight, preferred_element_type=F32).astype(BF16)
        if (i + 1) * pair * LANES % span == 0:
            q = (i + 1) * pair * LANES // span - 1
            part = span // narrow
            moved = jnp.dot(total[:, q * span : (q + 1) * span], mover[...], preferred_element_type=F32)
            for n in range(narrow):
                chunks[n, :, q * part : (q + 1) * part] = moved[:, n * part : (n + 1) * part].astype(BF16)
    if small:
        bc_copy.wait()
        dt_copy.wait()
        bc_part = jnp.dot(x, bc_held[...], preferred_element_type=F32)
        dt_part = lax.dot_general(x, dt_held[...], (((1,), (1,)), ((), ())), preferred_element_type=F32)
        chunk_cols, cols = chunks.shape[2], outs[0].shape[1]
        pad = jnp.zeros((rows, 2 * (cols - chunk_cols) - bc_part.shape[1] - dt_part.shape[1]), F32)
        sums = jnp.concatenate([bc_part, dt_part, pad], axis=1).astype(BF16)
        for mask in range(narrow):
            outs[mask][:rows, chunk_cols:] = sums[:, : cols - chunk_cols]
            outs[mask][rows:, chunk_cols:] = sums[:, cols - chunk_cols :]
    for mask in range(narrow):
        outs[mask][:, : chunks.shape[2]] = chunks[me_ref[1] ^ mask]
    for j in range(parts):
        later_copy(j).wait()


def proj(me, weight, inputs, given, half, narrow, chan, first, blocks, small, slots):
    feats, _, cols = weight.shape
    rows = inputs.shape[1] * half
    pair = 2 if blocks % 2 == 0 else 1
    slots = min(slots, blocks // pair)
    span = min(narrow, blocks) * LANES
    by_block = weight.reshape(feats, 2, cols // LANES, LANES).transpose(0, 2, 1, 3)
    cols = blocks * LANES // narrow
    scratch = [
        pltpu.VMEM((slots, pair, feats, 2, LANES), BF16),
        pltpu.VMEM((2, pair * 2 * feats, LANES), BF16),
        pltpu.VMEM(inputs.shape, BF16),
        pltpu.VMEM((2 * rows, 2 * feats), BF16),
        pltpu.VMEM((span, span), BF16),
        pltpu.VMEM((2 * rows, blocks * LANES), BF16),
        pltpu.VMEM((narrow, 2 * rows, blocks * LANES // narrow), BF16),
        pltpu.SemaphoreType.DMA((slots, pair)),
        pltpu.SemaphoreType.DMA((2,)),
        pltpu.SemaphoreType.DMA,
    ]
    specs = [VMEM_SPEC] * len(given)
    nbytes = 4 * feats * blocks * LANES
    if small:
        bc_weight, dt_weight_t = given
        out_shape = []
        cols += -(-(bc_weight.shape[1] + dt_weight_t.shape[0]) // (2 * LANES)) * LANES
        scratch += [pltpu.VMEM(value.shape, BF16) for value in given] + [pltpu.SemaphoreType.DMA] * 2
        specs = [HBM_SPEC] * 2
        nbytes += 2 * (bc_weight.size + dt_weight_t.size)
    else:
        history, later = given[0], given[-1]
        specs[-1] = HBM_SPEC
        nbytes += later.size * later.dtype.itemsize
        scratch += [pltpu.SemaphoreType.DMA((later.shape[0],))]
        out_shape = [jax.ShapeDtypeStruct(later.shape, later.dtype)]
        out_shape += [jax.ShapeDtypeStruct((3 * half + 8, history.shape[2] * history.shape[3]), BF16)]
    out_shape += [jax.ShapeDtypeStruct((2 * rows, cols), BF16)] * narrow
    return pl.pallas_call(
        functools.partial(
            proj_kernel, slots=slots, first=first, narrow=narrow, chan=chan, half=half, small=small
        ),
        out_shape=out_shape,
        in_specs=[SMEM_SPEC, HBM_SPEC, HBM_SPEC] + specs,
        out_specs=[VMEM_SPEC] * len(out_shape),
        scratch_shapes=scratch,
        compiler_params=params(PROJ_MIB if small else NEXT_PROJ_MIB),
        cost_estimate=cost(rows * nbytes, nbytes),
        name="proj_small" if small else "proj",
    )(me, by_block, inputs, *given)


def conv_pair(history, fresh, taps, offset):
    window = list(history) + list(fresh)
    outputs = []
    for token in range(2):
        summed = offset
        for tap in range(4):
            summed = summed + taps[tap : tap + 1] * window[token + tap]
        outputs.append(silu(summed))
    return outputs


def summed_refs(refs):
    total = refs[0][...].astype(F32)
    for ref in refs[1:]:
        total = total + ref[...].astype(F32)
    return total


def bc_conv_kernel(*refs, parts, seqs):
    history_ref, taps_ref, offset_ref, conv_ref, kept_ref, dt_ref, chan_ref = refs[parts:]
    rows, chunk_cols = conv_ref.shape[0], chan_ref.shape[1]
    both = summed_refs(refs[:parts])
    chan_ref[...] = both[:, :chunk_cols].astype(BF16)
    summed = jnp.concatenate([both[:rows, chunk_cols:], both[rows:, chunk_cols:]], axis=1)
    half = summed.shape[0] // 2
    cols = taps_ref.shape[1]
    proj = summed.astype(BF16).astype(F32)
    dt_ref[...] = proj[:, cols : cols + LANES]
    fresh = [proj[:seqs, :cols], proj[half : half + seqs, :cols]]
    history = [history_ref[i].astype(F32) for i in range(3)]
    conv_ref[...] = jnp.zeros_like(conv_ref)
    for token, value in enumerate(conv_pair(history, fresh, taps_ref[...].astype(F32), offset_ref[...].astype(F32))):
        conv_ref[token * half : token * half + seqs] = value
    kept_ref[0] = history_ref[2]
    kept_ref[1] = fresh[0].astype(BF16)
    kept_ref[2] = fresh[1].astype(BF16)


def bc_conv(parts, history, taps, offset, chunk_cols):
    rows = parts[0].shape[0]
    cols = taps.shape[1]
    return pl.pallas_call(
        functools.partial(bc_conv_kernel, parts=len(parts), seqs=history.shape[1]),
        out_shape=(
            jax.ShapeDtypeStruct((rows // 2, cols), F32),
            jax.ShapeDtypeStruct(history.shape, BF16),
            jax.ShapeDtypeStruct((rows // 2, LANES), F32),
            jax.ShapeDtypeStruct((rows, chunk_cols), BF16),
        ),
        in_specs=[VMEM_SPEC] * (len(parts) + 3),
        out_specs=(VMEM_SPEC,) * 4,
        compiler_params=params(8),
        cost_estimate=cost(30 * rows * cols, 8 * rows * cols),
        name="bc_conv",
    )(*parts, history, taps, offset)


def state_read_kernel(bc_ref, state_ref, read_ref, *, groups):
    seqs, rows, _ = state_ref.shape
    half = bc_ref.shape[0] // 2
    span = rows // groups
    read_ref[...] = jnp.zeros_like(read_ref)
    for seq in range(seqs):
        for g in range(groups):
            cols = slice((2 * g + 1) * STATE, (2 * g + 2) * STATE)
            both = jnp.concatenate([bc_ref[t * half + seq : t * half + seq + 1, cols] for t in range(2)], axis=0)
            held = state_ref[seq, g * span : (g + 1) * span].astype(BF16)
            out = lax.dot_general(both.astype(BF16), held, (((1,), (1,)), ((), ())), preferred_element_type=F32)
            for t in range(2):
                read_ref[t * half + seq : t * half + seq + 1, g * span : (g + 1) * span] = out[t : t + 1]


def state_read(bc, state, groups):
    seqs, rows, _ = state.shape
    return pl.pallas_call(
        functools.partial(state_read_kernel, groups=groups),
        out_shape=jax.ShapeDtypeStruct((bc.shape[0], rows), F32),
        in_specs=[VMEM_SPEC, VMEM_SPEC],
        out_specs=VMEM_SPEC,
        compiler_params=params(READ_MIB),
        cost_estimate=cost(4 * state.size, 4 * state.size),
        name="state_read",
    )(bc, state)


def readout_kernel(*refs, parts, groups, heads, chan):
    done_ref, part_refs = refs[0], refs[1 : parts + 1]
    lanes_ref, read_ref, bc_ref, dt_ref, heads_ref = refs[parts + 1 : parts + 6]
    sent_ref, fresh_ref, scale_ref, decay_ref = refs[parts + 6 :]
    columns = [done_ref[...].astype(F32)]
    if part_refs:
        columns.append(summed_refs(part_refs).astype(BF16).astype(F32))
    proj = jnp.concatenate(columns, axis=1)
    half = proj.shape[0] // 4
    width = proj.shape[1]
    gates = [proj[:half], proj[half : 2 * half]]
    fresh = [proj[2 * half : 3 * half], proj[3 * half :]]
    fresh_ref[...] = proj[2 * half :].astype(BF16)
    lanes = lanes_ref[...].astype(F32)
    history = [lanes[i * half : (i + 1) * half] for i in range(3)]
    taps, offset, gain = (lanes[3 * half + i : 3 * half + j] for i, j in ((0, 4), (4, 5), (5, 6)))
    x = conv_pair(history, fresh, taps, offset)

    bias, rate, skip = heads_ref[0:1], jnp.exp(heads_ref[1:2]), heads_ref[2:3]
    raw = dt_ref[:, :heads] + bias
    step = jnp.maximum(raw, 0.0) + jnp.log1p(jnp.exp(-jnp.abs(raw)))
    decay = jnp.exp(-step * rate)
    decay_ref[...] = decay[:half] * decay[half:]
    repeat = (iota((heads, width), 1) // chan == iota((heads, width), 0)).astype(F32)
    packed = jnp.concatenate([step, decay, jnp.broadcast_to(skip, (8, heads))], axis=0)
    spread = jnp.dot(packed, repeat, preferred_element_type=F32, precision=lax.Precision.HIGHEST)
    steps = [spread[:half], spread[half : 2 * half]]
    decays = [spread[2 * half : 3 * half], spread[3 * half : 4 * half]]
    skips = spread[4 * half : 4 * half + 1]

    span = width // groups

    def dots(b_token, c_token):
        out = []
        for g in range(groups):
            b = bc_ref[b_token * half : (b_token + 1) * half, 2 * g * STATE : (2 * g + 1) * STATE]
            c = bc_ref[c_token * half : (c_token + 1) * half, (2 * g + 1) * STATE : (2 * g + 2) * STATE]
            out.append(jnp.broadcast_to(jnp.sum(b * c, axis=1, keepdims=True), (half, span)))
        return jnp.concatenate(out, axis=1)

    first = steps[0] * x[0]
    second = steps[1] * x[1]
    carried = decays[1] * first
    y = [
        decays[0] * read_ref[:half] + first * dots(0, 0) + skips * x[0],
        decays[0] * decays[1] * read_ref[half:] + carried * dots(0, 1) + second * dots(1, 1) + skips * x[1],
    ]
    scale_ref[:half] = carried
    scale_ref[half:] = second
    lane = iota((half, LANES), 1)
    for token in range(2):
        gated = y[token] * silu(gates[token])
        rows = slice(token * half, (token + 1) * half)
        sent_ref[rows, :width] = (gated * gain).astype(BF16)
        squares = jnp.zeros((half, LANES), F32)
        for g in range(groups):
            part = gated[:, g * span : (g + 1) * span]
            total = jnp.sum(part * part, axis=1, keepdims=True)
            high = total.astype(BF16).astype(F32)
            squares = squares + jnp.where(lane == 2 * g, high, 0.0) + jnp.where(lane == 2 * g + 1, total - high, 0.0)
        sent_ref[rows, width:] = squares.astype(BF16)


def readout(done, parts, lanes, read, bc, dt, head_vals, groups, chan):
    rows, width = read.shape
    heads = head_vals.shape[1]
    return pl.pallas_call(
        functools.partial(readout_kernel, parts=len(parts), groups=groups, heads=heads, chan=chan),
        out_shape=(
            jax.ShapeDtypeStruct((rows, width + LANES), BF16),
            jax.ShapeDtypeStruct((rows, width), BF16),
            jax.ShapeDtypeStruct((rows, width), F32),
            jax.ShapeDtypeStruct((rows // 2, heads), F32),
        ),
        in_specs=[VMEM_SPEC] * (len(parts) + 6),
        out_specs=(VMEM_SPEC,) * 4,
        compiler_params=params(16),
        cost_estimate=cost(100 * rows * width, 12 * rows * width),
        name="readout",
    )(done, *parts, lanes, read, bc, dt, head_vals)


def state_write_kernel(*refs, groups, heads, first, count, prepare):
    if prepare:
        scale_ref, decay_ref, bc_ref, state_ref, new_ref, left, decays = refs[:7]
        refs = refs[7:]
    else:
        left, decays, bc_ref, state_ref, _, _, new_ref, mark_ref = refs[:8]
        refs = refs[8:]
        mark_ref[...] = jnp.zeros_like(mark_ref)
    right, made, sems = refs
    seqs, rows, _ = state_ref.shape
    half = bc_ref.shape[0] // 2
    span = rows // groups
    chan = rows // heads
    slots = made.shape[0]
    right[...] = jnp.zeros_like(right)
    if prepare:
        scale = scale_ref[...]
        high = scale.astype(BF16).astype(F32)
        pad = jnp.zeros((left.shape[1] - 6 * half, rows), F32)
        left[...] = jnp.concatenate([high, scale - high, high, pad], axis=0).T.astype(BF16)
        by_head = decay_ref[...].T
        for s in range(seqs):
            decays[s * heads : (s + 1) * heads] = jnp.broadcast_to(by_head[:, s : s + 1], (heads, LANES))

    def out_copy(seq):
        slot = (seq - first) % slots
        return pltpu.make_async_copy(made.at[slot], new_ref.at[seq], sems.at[slot])

    for seq in range(first, first + count):
        slot = (seq - first) % slots
        side = (seq - first) % right.shape[0]
        values = []
        for t in range(2):
            row = bc_ref[t * half + seq : t * half + seq + 1, :]
            values.append(jnp.concatenate([row[:, 2 * g * STATE : (2 * g + 1) * STATE] for g in range(groups)], axis=1))
        high = [value.astype(BF16).astype(F32) for value in values]
        low = [value - top for value, top in zip(values, high)]
        for block, value in enumerate(high + high + low):
            right[side, block * half + seq : block * half + seq + 1, :] = value
        if seq - first >= slots:
            out_copy(seq - slots).wait()
        for g in range(groups):
            here = slice(g * span, (g + 1) * span)
            factor = right[side, :, g * STATE : (g + 1) * STATE].astype(BF16)
            added = jnp.dot(left[here], factor, preferred_element_type=F32)
            for h in range(span // chan):
                head = g * (span // chan) + h
                decay = decays[seq * heads + head : seq * heads + head + 1, :]
                decay = jnp.concatenate([decay] * (STATE // LANES), axis=1)
                made[slot, head * chan : (head + 1) * chan] = (
                    decay * state_ref[seq, head * chan : (head + 1) * chan] + added[h * chan : (h + 1) * chan]
                )
        out_copy(seq).start()
        for block in range(6):
            right[side, block * half + seq : block * half + seq + 1, :] = jnp.zeros((1, right.shape[2]), F32)
    for seq in range(max(first, first + count - slots), first + count):
        out_copy(seq).wait()


def state_write(given, bc, state, groups, heads, first, count, before=None, after=None):
    seqs, rows, _ = state.shape
    half = bc.shape[0] // 2
    prepare = before is None
    depth = -(-6 * half // LANES) * LANES
    scratch = [
        pltpu.VMEM((2, depth, groups * STATE), F32),
        pltpu.VMEM((3, rows, STATE), F32),
        pltpu.SemaphoreType.DMA((3,)),
    ]
    if prepare:
        more = [
            jax.ShapeDtypeStruct((rows, depth), BF16),
            jax.ShapeDtypeStruct((seqs * heads, LANES), F32),
        ]
        extra = []
    else:
        more = [jax.ShapeDtypeStruct((8, LANES), F32)]
        extra = [before, after]
    nbytes = 4 * count * rows * STATE
    return pl.pallas_call(
        functools.partial(
            state_write_kernel, groups=groups, heads=heads, first=first, count=count, prepare=prepare
        ),
        out_shape=[jax.ShapeDtypeStruct(state.shape, F32)] + more,
        in_specs=[VMEM_SPEC] * 4 + [HBM_SPEC] * len(extra),
        out_specs=[HBM_SPEC] + [VMEM_SPEC] * len(more),
        scratch_shapes=scratch,
        input_output_aliases={} if prepare else {4: 0},
        compiler_params=params(WRITE_MIB),
        cost_estimate=cost(nbytes, 2 * nbytes),
        name="state_write",
    )(*given, bc, state, *extra)


def squares_kernel(me_ref, *refs, wide, groups):
    sent, out_ref = refs[:wide], refs[-1]
    rows, lanes = out_ref.shape
    lane = iota((rows, lanes), 1)
    total = jnp.zeros((rows, lanes), F32)
    for mask in range(wide):
        owner = me_ref[0] ^ mask
        value = sent[mask][:, sent[mask].shape[1] - lanes :].astype(F32)
        for g in range(groups):
            own = value[:, 2 * g : 2 * g + 1] + value[:, 2 * g + 1 : 2 * g + 2]
            total = total + jnp.where(lane == owner * groups + g, own, 0.0)
    out_ref[...] = total


def all_squares(me, sent, groups, after):
    wide = len(sent)
    return pl.pallas_call(
        functools.partial(squares_kernel, wide=wide, groups=groups),
        out_shape=jax.ShapeDtypeStruct((sent[0].shape[0], LANES), F32),
        in_specs=[SMEM_SPEC] + [VMEM_SPEC] * wide + [ANY_SPEC],
        out_specs=VMEM_SPEC,
        compiler_params=params(8),
        cost_estimate=cost(LANES * LANES * wide, 4 * LANES * LANES * wide),
        name="all_squares",
    )(me, *sent, after)


def out_proj_kernel(me_ref, *refs, wide, groups):
    sent = refs[:wide]
    w_ref, _, made_ref, held, sems = refs[wide:]
    width = w_ref.shape[0] // wide
    span = width // groups

    def copy(mask, g):
        owner = me_ref[0] ^ mask
        rows = pl.ds(pl.multiple_of(owner * width + g * span, span), span)
        return pltpu.make_async_copy(w_ref.at[rows], held.at[mask, pl.ds(g * span, span)], sems.at[mask, g])

    for mask in range(wide):
        for g in range(groups):
            copy(mask, g).start()
    for mask in range(wide):
        for g in range(groups):
            copy(mask, g).wait()
            rows = slice(g * span, (g + 1) * span)
            product = jnp.dot(sent[mask][:, rows], held[mask, rows], preferred_element_type=F32)
            made_ref[mask * groups + g] = product


def out_proj(me, sent, weight, groups, after):
    wide = len(sent)
    rows = sent[0].shape[0]
    depth, cols = weight.shape
    return pl.pallas_call(
        functools.partial(out_proj_kernel, wide=wide, groups=groups),
        out_shape=jax.ShapeDtypeStruct((wide * groups, rows, cols), F32),
        in_specs=[SMEM_SPEC] + [VMEM_SPEC] * wide + [HBM_SPEC, ANY_SPEC],
        out_specs=VMEM_SPEC,
        scratch_shapes=[pltpu.VMEM((wide, depth // wide, cols), BF16), pltpu.SemaphoreType.DMA((wide, groups))],
        compiler_params=params(OUT_MIB),
        cost_estimate=cost(2 * rows * depth * cols, 2 * depth * cols),
        name="out_proj",
    )(me, *sent, weight, after)


def out_scale_kernel(me_ref, made_ref, *refs, wide, narrow, groups, group_span):
    squares, outs, chunks = refs[:narrow], refs[narrow : 2 * narrow], refs[-1]
    summed = summed_refs(squares)
    lane = iota(summed.shape, 1)
    total = None
    for mask in range(wide):
        owner = me_ref[0] ^ mask
        for g in range(groups):
            low = (owner // group_span * group_span) * groups + g
            mine = (lane >= low) & (lane < low + (group_span - 1) * groups + 1)
            group_sum = jnp.sum(jnp.where(mine, summed, 0.0), axis=1, keepdims=True)
            inverse = lax.rsqrt(group_sum / (HEADS // NGROUPS * HEAD_DIM) + EPSILON)
            scaled = made_ref[mask * groups + g] * inverse
            total = scaled if total is None else total + scaled
    cols = total.shape[1] // narrow
    for n in range(narrow):
        chunks[n] = total[:, n * cols : (n + 1) * cols].astype(BF16)
    for mask in range(narrow):
        outs[mask][...] = chunks[me_ref[1] ^ mask]


def out_scale(me, made, squares, wide, groups, group_span):
    narrow = len(squares)
    _, rows, cols = made.shape
    return pl.pallas_call(
        functools.partial(out_scale_kernel, wide=wide, narrow=narrow, groups=groups, group_span=group_span),
        out_shape=[jax.ShapeDtypeStruct((rows, cols // narrow), BF16)] * narrow,
        in_specs=[SMEM_SPEC] + [VMEM_SPEC] * (narrow + 1),
        out_specs=[VMEM_SPEC] * narrow,
        scratch_shapes=[pltpu.VMEM((narrow, rows, cols // narrow), BF16)],
        compiler_params=params(8),
        cost_estimate=cost(4 * made.size, 4 * made.size),
        name="out_scale",
    )(me, made, *squares)


def shards(
    inputs,
    xz_weight,
    bc_weight,
    dt_weight,
    conv_x_weight,
    conv_x_bias,
    conv_bc_weight,
    conv_bc_bias,
    conv_x_state,
    conv_bc_state,
    dt_bias,
    a_log,
    d_skip,
    norm_weight,
    out_weight,
    ssm_state,
):
    seqs = inputs.shape[0]
    feats = inputs.shape[2]
    heads = dt_weight.shape[1]
    wide = lax.axis_size("wide")
    narrow = lax.axis_size("narrow")
    chan = HEAD_DIM // narrow
    width = heads * chan
    half = -(-seqs // 8) * 8
    groups = max(NGROUPS // wide, 1)
    group_span = max(wide // NGROUPS, 1)
    me = jnp.stack([lax.axis_index("wide"), lax.axis_index("narrow")]).astype(jnp.int32)

    blocks = xz_weight.shape[2] // LANES
    cut = blocks // 2
    state = ssm_state.reshape(seqs, width, STATE)
    given = (bc_weight, dt_weight.T)
    chunks = proj(me, xz_weight, inputs, given, half, narrow, chan, 0, cut, True, 3)
    early_parts = [chunks[0]] + [exchanged(chunks[mask], "narrow", mask) for mask in range(1, narrow)]
    history = conv_x_state.transpose(0, 1, 3, 2)
    given = (history, conv_x_weight.transpose(0, 2, 1), conv_x_bias.T, norm_weight.T, state)
    state, lanes, *chunks = proj(me, xz_weight, inputs, given, half, narrow, chan, cut, blocks - cut, False, 4)
    late_parts = [chunks[0]] + [exchanged(chunks[mask], "narrow", mask) for mask in range(1, narrow)]

    conv, kept_bc, dt, early_done = bc_conv(
        early_parts, conv_bc_state.transpose(1, 0, 2), conv_bc_weight, conv_bc_bias.reshape(1, -1), chunks[0].shape[1]
    )
    for bit in range(group_span.bit_length() - 1):
        partner = exchanged(conv.astype(BF16), "wide", 1 << bit).astype(F32)
        is_lower = lax.axis_index("wide") // (1 << bit) % 2 == 0
        conv = jnp.where(
            is_lower, jnp.concatenate([conv, partner], axis=1), jnp.concatenate([partner, conv], axis=1)
        )

    read = state_read(conv, state, groups)

    sent, fresh, scale, decay = readout(
        early_done,
        late_parts,
        lanes,
        read,
        conv,
        dt,
        jnp.stack([dt_bias, a_log, d_skip]),
        groups,
        chan,
    )

    gathered = from_all(sent, "wide")
    early = seqs * 4 // 5
    new_state, left, decays = state_write((scale, decay), conv, state, groups, heads, 0, early)
    squares = all_squares(me, gathered, groups, left)
    square_list = from_all(squares, "narrow")
    made = out_proj(me, gathered, out_weight.reshape(-1, out_weight.shape[2]), groups, squares)
    out_chunks = out_scale(me, made, square_list, wide, groups, group_span)
    new_state, _ = state_write(
        (left, decays), conv, state, groups, heads, early, seqs - early, new_state, out_chunks[0]
    )
    out_sum = out_chunks[0].astype(F32)
    for mask in range(1, narrow):
        out_sum = out_sum + exchanged(out_chunks[mask], "narrow", mask).astype(F32)
    layer_out = out_sum.astype(BF16).reshape(2, half, -1)[:, :seqs].transpose(1, 0, 2)

    new_conv_x = kept_channels(history, fresh).transpose(0, 1, 3, 2)
    return (layer_out, new_state.reshape(ssm_state.shape), new_conv_x, kept_bc.transpose(1, 0, 2))


def solution(mesh):
    return jax.shard_map(
        shards,
        mesh=mesh,
        in_specs=(
            P("groups", None, "narrow"),
            P("narrow", None, "wide"),
            P("narrow", "wide"),
            P("narrow", "wide"),
            P(None, "wide", "narrow"),
            P("wide", "narrow"),
            P(None, "wide"),
            P("wide"),
            P("groups", None, "wide", "narrow"),
            P("groups", None, "wide"),
            P("wide"),
            P("wide"),
            P("wide"),
            P("wide", "narrow"),
            P(None, "narrow", "wide"),
            P("groups", "wide", "narrow", None),
        ),
        out_specs=(
            P("groups", None, ("wide", "narrow")),
            P("groups", "wide", "narrow", None),
            P("groups", None, "wide", "narrow"),
            P("groups", None, "wide"),
        ),
        check_vma=False,
    )
```
